512 devices in a mesh: seq: 32 (over x, z_lo), pass: 2 (over core), head: 8 (over z_hi, y).
Axes of the slice: x: 4, y: 4, z: 16 (z_hi: 2, z_lo: 8; z = z_hi * 8 + z_lo), core: 2. Of those that a mesh axis runs over, the one named last changes fastest.
Arguments:
- queries: bfloat16 [2, 4096, 3072], P('pass', 'seq', 'head'), may hold values from -8 to 8
- keys: bfloat16 [2, 4096, 3072], P('pass', 'seq', 'head'), may hold values from -8 to 8
- values: bfloat16 [2, 4096, 3072], P('pass', 'seq', 'head'), may hold values from -6 to 6
- self_pairs: int32 [2, 160, 2], replicated, may hold values from 0 to 31, as said below
- mask_pairs: int32 [128, 2], replicated, may hold values from 0 to 31, as said below
- counts: int32 [3], replicated, may hold values from 32 to 160, as said below
- out_weight: bfloat16 [3072, 3072], P('head'), may hold values from -0.109375 to 0.109375
Outputs:
- projected: bfloat16 [2, 4096, 3072], P('pass', 'seq', 'head')
The draws below stay inside these ranges and needn't reach their ends.
Inputs may be any that keep to these rules, and one draw needn't show every extreme that they name: `self_pairs`: tile numbers. In each pass's list the first 32 entries are (t, t) for t = 0 to 31; the first counts[p] entries are live, the rest are padding; pairs may repeat. `mask_pairs`: tile numbers; the first counts[2] entries are live; pairs may repeat. counts[0] and counts[1] lie between 32 and 160, and one of them is 160; counts[2] lies between 64 and 128.
All inputs are finite; a program needn't handle non-finite values.
Results may differ from the reference program's by a relative error of at most 0.01.
Values may be sent and summed in bfloat16 or wider, within the bound.
A program may use at most 64 MiB of HBM per device.

```python
import jax
import jax.numpy as jnp
from jax import lax

D = 3072
HEADS = 24
HD = 128
TILE = 128
TOKENS = 4096
NT = 32
LIST = 160
MLIST = 128


def skewed_tiles(key, shape):
    first_key, second_key, third_key, order_key = jax.random.split(key, 4)
    lowest = jnp.minimum(jax.random.randint(first_key, shape, 0, NT), jax.random.randint(second_key, shape, 0, NT))
    lowest = jnp.minimum(lowest, jax.random.randint(third_key, shape, 0, NT))
    order = jax.random.permutation(order_key, NT).astype(jnp.int32)
    return order[lowest]


def draw_queries(key, part):
    key = jax.random.fold_in(key, 11)
    base_key = jax.random.fold_in(key, 0)
    result = 1.5 * jax.random.truncated_normal(base_key, -5.0, 5.0, (2, TOKENS, D))
    return result.astype(jnp.bfloat16)


def draw_keys(key, part):
    key = jax.random.fold_in(key, 13)
    base_key = jax.random.fold_in(key, 0)
    result = jax.random.truncated_normal(base_key, -6.0, 6.0, (2, TOKENS, D))
    return result.astype(jnp.bfloat16)


def draw_self_pairs(key, part):
    key = jax.random.fold_in(key, 21)
    lists = []
    for pass_number in range(2):
        pass_key = jax.random.fold_in(key, pass_number)
        query_key, target_key = jax.random.split(pass_key)
        diagonal = jnp.arange(NT, dtype=jnp.int32)
        query_tiles = jnp.concatenate([diagonal, skewed_tiles(query_key, (LIST - NT,))])
        key_tiles = jnp.concatenate([diagonal, jax.random.randint(target_key, (LIST - NT,), 0, NT)])
        lists.append(jnp.stack([query_tiles, key_tiles], axis=1))
    return jnp.stack(lists).astype(jnp.int32)


def draw_mask_pairs(key, part):
    key = jax.random.fold_in(key, 27)
    query_key, target_key = jax.random.split(key)
    query_tiles = skewed_tiles(query_key, (MLIST,))
    key_tiles = jax.random.randint(target_key, (MLIST,), 0, NT)
    return jnp.stack([query_tiles, key_tiles], axis=1).astype(jnp.int32)


def draw_counts(key, part):
    key = jax.random.fold_in(key, 31)
    choose_key, other_key, cross_key = jax.random.split(key, 3)
    flipped = jax.random.randint(choose_key, (), 0, 2)
    another = jax.random.randint(other_key, (), NT, LIST + 1)
    first_count = jnp.where(flipped == 0, LIST, another)
    second_count = jnp.where(flipped == 0, another, LIST)
    cross_count = jax.random.randint(cross_key, (), MLIST // 2, MLIST + 1)
    return jnp.stack([first_count, second_count, cross_count]).astype(jnp.int32)


def level_of(stream_key, dims, cuts, least, high):
    loudness = 1.0
    for axis_at, parts in cuts:
        steps = jax.random.uniform(jax.random.fold_in(jax.random.fold_in(stream_key, 6), axis_at), (parts,), jnp.float32, least / len(cuts), high / len(cuts))
        loudness = loudness * jnp.repeat(jnp.exp(steps), dims[axis_at] // parts).reshape((-1,) + (1,) * (len(dims) - 1 - axis_at))
    return loudness


def scatter_about(stream_key, extent, scale, reach, cuts=(), held_as=jnp.bfloat16):
    values = scale * jax.random.normal(stream_key, extent, jnp.float32)
    if cuts:
        values = values * level_of(stream_key, extent, cuts, -0.22, 0.18)
    return jnp.clip(values, -reach, reach).astype(held_as)


def setup_inputs(seed: int = 0) -> dict:
    streams_of = jax.random.split(jax.random.key(seed), 8)
    queries = draw_queries(jax.random.fold_in(streams_of[7], 71), 0)
    keys = draw_keys(jax.random.fold_in(streams_of[7], 71), 0)
    values = scatter_about(streams_of[2], (2, TOKENS, D), 1.0, 6.0, ((0, 2), (1, 32), (2, 8)))
    self_pairs = draw_self_pairs(jax.random.fold_in(streams_of[7], 71), 0)
    mask_pairs = draw_mask_pairs(jax.random.fold_in(streams_of[7], 71), 0)
    counts = draw_counts(jax.random.fold_in(streams_of[7], 71), 0)
    out_weight = scatter_about(streams_of[6], (D, D), D ** -0.5, 0.109375, ((0, 8),))
    return {"queries": queries, "keys": keys, "values": values, "self_pairs": self_pairs, "mask_pairs": mask_pairs, "counts": counts, "out_weight": out_weight}


NEG_FILL = -1e30


def tile_table(pairs, live_count):
    entries = jnp.arange(pairs.shape[0], dtype=jnp.int32)
    tiles = jnp.arange(NT, dtype=jnp.int32)
    live = entries < live_count
    row_hits = ((pairs[:, 0][:, None] == tiles[None, :]) & live[:, None]).astype(jnp.float32)
    col_hits = (pairs[:, 1][:, None] == tiles[None, :]).astype(jnp.float32)
    return jnp.dot(row_hits.T, col_hits) > 0.5


def expand_table(table):
    return jnp.repeat(jnp.repeat(table, TILE, axis=0), TILE, axis=1)


def split_heads(array):
    return jnp.transpose(array.reshape(TOKENS, HEADS, HD), (1, 0, 2))


def head_attention(query_head, key_head, value_head, source_key, source_value, self_mask, cross_mask):
    scale_factor = HD ** -0.5
    self_scores = jnp.dot(query_head, key_head.T, preferred_element_type=jnp.float32) * scale_factor
    cross_scores = jnp.dot(query_head, source_key.T, preferred_element_type=jnp.float32) * scale_factor
    self_scores = jnp.where(self_mask, self_scores, NEG_FILL)
    cross_scores = jnp.where(cross_mask, cross_scores, NEG_FILL)
    row_max = jnp.maximum(jnp.max(self_scores, axis=1), jnp.max(cross_scores, axis=1))
    self_exp = jnp.where(self_mask, jnp.exp(self_scores - row_max[:, None]), 0.0)
    cross_exp = jnp.where(cross_mask, jnp.exp(cross_scores - row_max[:, None]), 0.0)
    row_total = jnp.sum(self_exp, axis=1) + jnp.sum(cross_exp, axis=1)
    mixed = jnp.dot(self_exp.astype(jnp.bfloat16), value_head, preferred_element_type=jnp.float32)
    mixed = mixed + jnp.dot(cross_exp.astype(jnp.bfloat16), source_value, preferred_element_type=jnp.float32)
    return (mixed / row_total[:, None]).astype(jnp.bfloat16)


def reference(queries, keys, values, self_pairs, mask_pairs, counts, out_weight):
    cross_full = expand_table(tile_table(mask_pairs, counts[2]))
    source_keys = split_heads(keys[0])
    source_values = split_heads(values[0])
    results = []
    for pass_number in range(2):
        self_full = expand_table(tile_table(self_pairs[pass_number], counts[pass_number]))
        if pass_number == 1:
            cross_use = cross_full
        else:
            cross_use = jnp.zeros_like(cross_full)

        def per_head(operands):
            query_head, key_head, value_head, source_key, source_value = operands
            return head_attention(query_head, key_head, value_head, source_key, source_value, self_full, cross_use)

        attended = lax.map(per_head, (split_heads(queries[pass_number]), split_heads(keys[pass_number]), split_heads(values[pass_number]), source_keys, source_values))
        joined = jnp.transpose(attended, (1, 0, 2)).reshape(TOKENS, D)
        results.append(jnp.dot(joined, out_weight, preferred_element_type=jnp.float32).astype(jnp.bfloat16))
    return jnp.stack(results)
```

```python
import functools
import math

import jax
import jax.numpy as jnp
from jax import lax
from jax.experimental import pallas as pl
from jax.experimental.pallas import tpu as pltpu
from jax.sharding import PartitionSpec as P

HD = 128
TILE = 128
NX = 4
NZ = 8
NY = 4
NT = 32
SLOTS = 4
ENTRIES = 2 * NT
BF16 = jnp.bfloat16
F32 = jnp.float32
I32 = jnp.int32
EXP2_SCALE = HD ** -0.5 * math.log2(math.e)
MESH = pl.DeviceIdType.MESH


def head_of_row(z):
    return (3 * z + 1) // 8


def first_row(g):
    return (8 * g + 1) // 3


def last_row(g):
    return (8 * g + 9) // 3 - 1


def query_place(zq, g):
    if g == 0:
        return zq // 3, zq % 3
    if g == 1:
        return 3 + zq // 4, zq % 4
    return 7 - (7 - zq) // 3, (7 - zq) % 3


def slot_row(z, g, j):
    low = 3 * z + j
    mid = 4 * (z - 3) + j
    high = 7 - (3 * (7 - z) + j)
    row = jnp.where(g == 0, low, jnp.where(g == 1, mid, high))
    return jnp.where((j == 3) & (g != 1), -1, row)


def row_order(i, z):
    near = jnp.minimum(z, 7 - z)
    d = (i + 1) // 2
    both = z + d * (1 - 2 * (i % 2))
    return jnp.where(i <= 2 * near, both, jnp.where(z <= 3, i, 7 - i))


def gather_kernel(
    counts_ref, q_ref, k_ref, v_ref, sp_ref, mp_ref, w_ref,
    kv_ref, qs_ref, list_ref, w2_ref,
    mine, list_v,
    z_send, z_recv, zf_send, xr_send, xl_send, xl_recv, xr_recv,
    fk_send, fk_recv, fv_send, fv_recv, c_send, c_recv,
    q_send, q_recv, w_send, w_recv, wc_send, wc_recv, local_sem,
):
    s = lax.axis_index("seq")
    p = lax.axis_index("pass")
    h = lax.axis_index("head")
    x, z = s // NZ, s % NZ
    zh, y = h // NY, h % NY
    g = head_of_row(z)
    a, b = first_row(g), last_row(g)
    right = ((x + 1) % NX) * NZ + z
    left = ((x + 3) % NX) * NZ + z

    def dev(seq=s, core=p, head=h):
        return {"seq": seq, "pass": core, "head": head}

    barrier = pltpu.get_barrier_semaphore()
    for d in range(1, NZ):
        pl.semaphore_signal(barrier, inc=1, device_id=dev(seq=x * NZ + (z + d) % NZ), device_id_type=MESH)
    for d in range(1, NY):
        pl.semaphore_signal(barrier, inc=1, device_id=dev(head=zh * NY + (y + d) % NY), device_id_type=MESH)
    for seq in (right, left):
        pl.semaphore_signal(barrier, inc=1, device_id=dev(seq=seq), device_id_type=MESH)
    pl.semaphore_signal(barrier, inc=1, device_id=dev(core=1 - p), device_id_type=MESH)

    for n in range(3):
        cols = slice(n * HD, (n + 1) * HD)
        mine[n, :TILE, :] = k_ref[:, cols]
        mine[n, TILE:, :] = v_ref[:, cols].T

    pl.semaphore_wait(barrier, NZ - 1 + NY - 1 + 3)

    def remote(src, dst, send, recv, target):
        return pltpu.make_async_remote_copy(
            src_ref=src, dst_ref=dst, send_sem=send, recv_sem=recv, device_id=target, device_id_type=MESH
        )

    def entry_copy(n):
        e = jnp.maximum(first_row(n), jnp.minimum(z, last_row(n)))
        return e, remote(mine.at[n], kv_ref.at[s], z_send.at[n], z_recv.at[z], dev(seq=x * NZ + e))

    def up_copy(row_from, src, send):
        return remote(src, kv_ref.at[x * NZ + row_from], send, z_recv.at[row_from], dev(seq=s + 1))

    def down_copy(row_from, src, send):
        return remote(src, kv_ref.at[x * NZ + row_from], send, z_recv.at[row_from], dev(seq=s - 1))

    own_copy = pltpu.make_async_copy(mine.at[g], kv_ref.at[s], local_sem.at[0])
    own_copy.start()

    @pl.when(z < b)
    def _():
        up_copy(z, mine.at[g], z_send.at[3]).start()

    @pl.when(z > a)
    def _():
        down_copy(z, mine.at[g], z_send.at[4]).start()

    for n in range(3):
        e, copy = entry_copy(n)

        @pl.when(e != z)
        def _():
            copy.start()

    def query_copies(n):
        row, slot = query_place(z, n)
        src = q_ref.at[:, n * HD:(n + 1) * HD]
        away = remote(src, qs_ref.at[slot], q_send.at[n], q_recv.at[slot], dev(seq=x * NZ + row))
        here = pltpu.make_async_copy(src, qs_ref.at[slot], q_send.at[n])
        return row, away, here

    for n in range(3):
        row, away, here = query_copies(n)

        @pl.when(row != z)
        def _():
            away.start()

        @pl.when(row == z)
        def _():
            here.start()

    half_rows = 3 * HD // 2
    rows_mine = pl.ds(pl.multiple_of(p * half_rows, half_rows), half_rows)
    rows_other = pl.ds(pl.multiple_of((1 - p) * half_rows, half_rows), half_rows)

    def w_cols(yy, part):
        zz = zh if part == 0 else 1 - zh
        return pl.ds(pl.multiple_of((zz * NY + yy) * (3 * HD), 3 * HD), 3 * HD)

    def part_cols(part):
        return slice(part * 3 * HD, (part + 1) * 3 * HD)

    def w_copy(d, part):
        yy = (y + d) % NY
        return remote(
            w_ref.at[rows_mine, w_cols(yy, part)], w2_ref.at[y, rows_mine, part_cols(part)],
            w_send.at[2 * d + part], w_recv.at[2 * d + part], dev(head=zh * NY + yy),
        )

    def w_arrival(d, part):
        yy = (y + NY - d) % NY
        return remote(
            w_ref.at[rows_mine, w_cols(yy, part)], w2_ref.at[yy, rows_mine, part_cols(part)],
            w_send.at[2 * d + part], w_recv.at[2 * d + part], dev(head=zh * NY + yy),
        )

    def w_swap(d, rows):
        yy = (y + NY - d) % NY
        return remote(
            w2_ref.at[yy, rows], w2_ref.at[yy, rows], wc_send.at[d], wc_recv.at[d], dev(core=1 - p)
        )

    def w_local(part):
        return pltpu.make_async_copy(
            w_ref.at[:, w_cols(y, part)], w2_ref.at[y, :, part_cols(part)], local_sem.at[1 + part]
        )

    for part in range(2):
        w_local(part).start()
        for d in range(1, NY):
            w_copy(d, part).start()

    lane = lax.broadcasted_iota(I32, (1, 128), 1)
    tiles = jnp.full((1, 128), -1, I32)
    for j in range(SLOTS):
        row = slot_row(z, g, j)
        tile = jnp.where((row >= 0) & (row < NZ), x * NZ + row, -1)
        tiles = jnp.where(lane == j, tile, tiles)

    def hits(pairs, live_count, shift):
        live = lax.broadcasted_iota(I32, (pairs.shape[0], 1), 0) < live_count
        row_hits = ((pairs[:, 0:1] == tiles) & live).astype(F32)
        col_hits = (pairs[:, 1:2] + shift == lane).astype(F32)
        return lax.dot_general(row_hits, col_hits, (((0,), (0,)), ((), ())), preferred_element_type=F32)[:8]

    is_edit = (p == 1).astype(F32)
    total = hits(sp_ref[p], counts_ref[p], 0) + is_edit * hits(mp_ref[...], counts_ref[2], NT)
    allowed = (total > 0.5).astype(F32)
    earlier = lax.broadcasted_iota(I32, (128, 128), 0) < lax.broadcasted_iota(I32, (128, 128), 1)
    rank = jnp.dot(allowed, earlier.astype(F32), preferred_element_type=F32)
    lanes = lax.broadcasted_iota(I32, (8, 128), 1)
    lanes_f = lanes.astype(F32)
    picked = allowed * lanes_f
    listing = jnp.where(lanes == 127, jnp.sum(allowed, axis=1, keepdims=True), 0.0)

    def put(at, listing):
        found = jnp.sum(jnp.where(rank == at.astype(F32), picked, 0.0), axis=1, keepdims=True)
        return jnp.where(lanes == at, found, listing)

    listing = lax.fori_loop(0, ENTRIES, put, listing)
    list_v[...] = listing.astype(I32)
    list_copy = pltpu.make_async_copy(list_v, list_ref, local_sem.at[3])
    list_copy.start()

    def chip_copy(tile):
        return remote(kv_ref.at[tile], kv_ref.at[NT + tile], c_send.at[tile], c_recv.at[tile], dev(core=1 - p))

    def chip_start(tile):
        @pl.when(p == 0)
        def _():
            chip_copy(tile).start()

    def tile_at(dx, r):
        return ((x + dx) % NX) * NZ + r

    def right_copy(tile, r):
        return remote(kv_ref.at[tile], kv_ref.at[tile], xr_send.at[r], xl_recv.at[r], dev(seq=right))

    def left_copy(tile, r):
        return remote(kv_ref.at[tile], kv_ref.at[tile], xl_send.at[r], xr_recv.at[r], dev(seq=left))

    def key_copy(tile, r):
        part = kv_ref.at[tile, :TILE]
        return remote(part, part, fk_send.at[r], fk_recv.at[r], dev(seq=right))

    def value_copy(tile, r):
        part = kv_ref.at[tile, TILE:]
        return remote(part, part, fv_send.at[r], fv_recv.at[r], dev(seq=left))

    def step(i, carry):
        @pl.when(i < NZ)
        def _():
            r = row_order(i, z)
            tile = x * NZ + r

            @pl.when(r == z)
            def _():
                own_copy.wait()

            @pl.when(r != z)
            def _():
                remote(kv_ref.at[tile], kv_ref.at[tile], z_send.at[0], z_recv.at[r], dev(seq=s)).wait_recv()

            @pl.when((r < z) & (z < b))
            def _():
                up_copy(r, kv_ref.at[tile], zf_send.at[r]).start()

            @pl.when((r > z) & (z > a))
            def _():
                down_copy(r, kv_ref.at[tile], zf_send.at[r]).start()

            right_copy(tile, r).start()
            left_copy(tile, r).start()
            chip_start(tile)

        @pl.when((i >= 1) & (i <= NZ))
        def _():
            r = row_order(i - 1, z)
            from_left, from_right = tile_at(3, r), tile_at(1, r)
            right_copy(from_left, r).wait_recv()
            key_copy(from_left, r).start()
            chip_start(from_left)
            left_copy(from_right, r).wait_recv()
            value_copy(from_right, r).start()
            chip_start(from_right)

        @pl.when(i >= 2)
        def _():
            r = row_order(i - 2, z)
            far = tile_at(2, r)
            key_copy(far, r).wait_recv()
            value_copy(far, r).wait_recv()
            chip_start(far)

        return carry

    lax.fori_loop(0, NZ + 2, step, 0)

    for d in range(1, NY):
        for part in range(2):
            w_arrival(d, part).wait_recv()
        w_swap(d, rows_mine).start()

    def drain(r, carry):
        tile = x * NZ + r

        @pl.when((r < z) & (z < b))
        def _():
            up_copy(r, kv_ref.at[tile], zf_send.at[r]).wait_send()

        @pl.when((r > z) & (z > a))
        def _():
            down_copy(r, kv_ref.at[tile], zf_send.at[r]).wait_send()

        right_copy(tile, r).wait_send()
        left_copy(tile, r).wait_send()
        key_copy(tile_at(3, r), r).wait_send()
        value_copy(tile_at(1, r), r).wait_send()
        return carry

    lax.fori_loop(0, NZ, drain, 0)

    def drain_chip(t, carry):
        @pl.when(p == 0)
        def _():
            chip_copy(t).wait_send()

        @pl.when(p == 1)
        def _():
            chip_copy(t).wait_recv()

        return carry

    lax.fori_loop(0, NT, drain_chip, 0)

    @pl.when(z < b)
    def _():
        up_copy(z, mine.at[g], z_send.at[3]).wait_send()

    @pl.when(z > a)
    def _():
        down_copy(z, mine.at[g], z_send.at[4]).wait_send()

    for n in range(3):
        e, copy = entry_copy(n)

        @pl.when(e != z)
        def _():
            copy.wait_send()

        row, away, here = query_copies(n)

        @pl.when(row != z)
        def _():
            away.wait_send()

        @pl.when(row == z)
        def _():
            here.wait()

    for j in range(SLOTS):
        row = slot_row(z, g, j)

        @pl.when((row >= 0) & (row < NZ) & (row != z))
        def _():
            remote(
                q_ref.at[:, :HD], qs_ref.at[j], q_send.at[0], q_recv.at[j], dev(seq=s)
            ).wait_recv()

    list_copy.wait()
    for part in range(2):
        w_local(part).wait()
    for d in range(1, NY):
        for part in range(2):
            w_copy(d, part).wait_send()
        w_swap(d, rows_mine).wait_send()
        w_swap(d, rows_other).wait_recv()


def attention_kernel(list_ref, q_ref, kv_ref, o_ref, scores):
    def slot(j, carry):
        n = list_ref[j, 127]

        @pl.when(n > 0)
        def _():
            query = q_ref[j].T

            def score(i, top):
                t = list_ref[j, i]
                got = jnp.dot(kv_ref[t, :TILE, :], query, preferred_element_type=F32)
                scores[i] = got
                return jnp.maximum(top, jnp.max(got.reshape(16, 8, TILE), axis=0))

            top = lax.fori_loop(0, n, score, jnp.full((8, TILE), -3e38, F32))
            shift = jnp.max(top, axis=0, keepdims=True) * EXP2_SCALE

            def gather(i, state):
                total, acc = state
                t = list_ref[j, i]
                exps = jnp.exp2(scores[i] * EXP2_SCALE - shift)
                total = total + jnp.sum(exps.reshape(16, 8, TILE), axis=0)
                acc = acc + jnp.dot(kv_ref[t, TILE:, :], exps.astype(BF16), preferred_element_type=F32)
                return total, acc

            total, acc = lax.fori_loop(
                0, n, gather, (jnp.zeros((8, TILE), F32), jnp.zeros((HD, TILE), F32))
            )
            row_total = jnp.sum(total, axis=0, keepdims=True)
            o_ref[j] = (acc / row_total).T.astype(BF16)

        return carry

    lax.fori_loop(0, SLOTS, slot, 0)


def project_kernel(
    o_ref, w2_ref, out_ref,
    w_v, full, give, got,
    o_send, o_recv, y_send, y_recv, h_send, h_recv, local_sem,
):
    s = lax.axis_index("seq")
    p = lax.axis_index("pass")
    h = lax.axis_index("head")
    x, z = s // NZ, s % NZ
    zh, y = h // NY, h % NY
    g = head_of_row(z)
    partner = (1 - zh) * NY + y

    def dev(seq=s, head=h):
        return {"seq": seq, "pass": p, "head": head}

    w_copy = pltpu.make_async_copy(w2_ref, w_v, local_sem.at[0])
    w_copy.start()
    barrier = pltpu.get_barrier_semaphore()
    for d in range(1, NZ):
        pl.semaphore_signal(barrier, inc=1, device_id=dev(seq=x * NZ + (z + d) % NZ), device_id_type=MESH)
    for d in range(1, NY):
        pl.semaphore_signal(barrier, inc=1, device_id=dev(head=zh * NY + (y + d) % NY), device_id_type=MESH)
    pl.semaphore_signal(barrier, inc=1, device_id=dev(head=partner), device_id_type=MESH)
    pl.semaphore_wait(barrier, NZ - 1 + NY)

    def remote(src, dst, send, recv, target):
        return pltpu.make_async_remote_copy(
            src_ref=src, dst_ref=dst, send_sem=send, recv_sem=recv, device_id=target, device_id_type=MESH
        )

    def back(j):
        row = slot_row(z, g, j)
        live = (row >= 0) & (row < NZ)
        dst = full.at[3 * y + g]
        away = remote(o_ref.at[j], dst, o_send.at[j], o_recv.at[g], dev(seq=x * NZ + row))
        here = pltpu.make_async_copy(o_ref.at[j], dst, o_send.at[j])
        return row, live, away, here

    for j in range(SLOTS):
        row, live, away, here = back(j)

        @pl.when(live & (row != z))
        def _():
            away.start()

        @pl.when(live & (row == z))
        def _():
            here.start()

    def y_copy(n, d):
        block = full.at[3 * y + n]
        return remote(
            block, block, y_send.at[3 * n + d - 1], y_recv.at[3 * n + d - 1],
            dev(head=zh * NY + (y + d) % NY),
        )

    def y_arrival(n, d):
        block = full.at[3 * ((y + NY - d) % NY) + n]
        return remote(
            block, block, y_send.at[3 * n + d - 1], y_recv.at[3 * n + d - 1],
            dev(head=zh * NY + (y + d) % NY),
        )

    for j in range(SLOTS):
        row, live, away, here = back(j)

        @pl.when(live & (row == z))
        def _():
            here.wait()

    for n in range(3):
        row, _slot = query_place(z, n)
        block = full.at[3 * y + n]

        @pl.when(row != z)
        def _():
            remote(block, block, o_send.at[0], o_recv.at[n], dev(seq=s)).wait_recv()

        for d in range(1, NY):
            y_copy(n, d).start()

    w_copy.wait()
    for n in range(3):
        for d in range(1, NY):
            y_arrival(n, d).wait_recv()

    def projected(part):
        acc = jnp.zeros((TILE, 3 * HD), F32)
        for n in range(3 * NY):
            acc = acc + jnp.dot(
                full[n], w_v[n * HD:(n + 1) * HD, part * 3 * HD:(part + 1) * 3 * HD],
                preferred_element_type=F32,
            )
        return acc

    give[...] = projected(1).astype(BF16)
    swap = remote(give, got, h_send, h_recv, dev(head=partner))
    swap.start()
    own = projected(0)
    swap.wait_recv()
    out_ref[...] = (own + got[...].astype(F32)).astype(BF16)

    swap.wait_send()
    for j in range(SLOTS):
        row, live, away, here = back(j)

        @pl.when(live & (row != z))
        def _():
            away.wait_send()

    for n in range(3):
        for d in range(1, NY):
            y_copy(n, d).wait_send()


def on_device(queries, keys, values, self_pairs, mask_pairs, counts, out_weight):
    vmem = pl.BlockSpec(memory_space=pltpu.VMEM)
    smem = pl.BlockSpec(memory_space=pltpu.SMEM)
    hbm = pl.BlockSpec(memory_space=pl.ANY)
    dma = pltpu.SemaphoreType.DMA
    shape = jax.ShapeDtypeStruct
    big = 48 * 1024 * 1024

    tiles, slots, listing, weights = pl.pallas_call(
        gather_kernel,
        out_shape=(
            shape((ENTRIES, 2 * TILE, HD), BF16),
            shape((SLOTS, TILE, HD), BF16),
            shape((8, 128), I32),
            shape((NY, 3 * HD, 6 * HD), BF16),
        ),
        in_specs=[smem, vmem, vmem, vmem, vmem, vmem, hbm],
        out_specs=(hbm, hbm, hbm, hbm),
        scratch_shapes=[
            pltpu.VMEM((3, 2 * TILE, HD), BF16),
            pltpu.VMEM((8, 128), I32),
            dma((5,)), dma((NZ,)), dma((NZ,)),
            dma((NZ,)), dma((NZ,)), dma((NZ,)), dma((NZ,)),
            dma((NZ,)), dma((NZ,)), dma((NZ,)), dma((NZ,)),
            dma((NT,)), dma((NT,)),
            dma((3,)), dma((SLOTS,)),
            dma((2 * NY,)), dma((2 * NY,)), dma((NY,)), dma((NY,)), dma((4,)),
        ],
        compiler_params=pltpu.CompilerParams(collective_id=0, has_side_effects=True),
        name="gather_tiles",
    )(counts, queries[0], keys[0], values[0], self_pairs, mask_pairs, out_weight)

    attended = pl.pallas_call(
        attention_kernel,
        out_shape=shape((SLOTS, TILE, HD), BF16),
        in_specs=[smem, vmem, vmem],
        out_specs=vmem,
        scratch_shapes=[pltpu.VMEM((ENTRIES, TILE, TILE), F32)],
        compiler_params=pltpu.CompilerParams(vmem_limit_bytes=big),
        name="attention",
    )(listing, slots, tiles)

    projected = pl.pallas_call(
        project_kernel,
        out_shape=shape((TILE, 3 * HD), BF16),
        in_specs=[vmem, hbm],
        out_specs=vmem,
        scratch_shapes=[
            pltpu.VMEM((3 * NY * HD, 6 * HD), BF16),
            pltpu.VMEM((3 * NY, TILE, HD), BF16),
            pltpu.VMEM((TILE, 3 * HD), BF16),
            pltpu.VMEM((TILE, 3 * HD), BF16),
            dma((SLOTS,)), dma((3,)), dma((9,)), dma((9,)), dma, dma, dma((1,)),
        ],
        compiler_params=pltpu.CompilerParams(collective_id=1, has_side_effects=True, vmem_limit_bytes=big),
        name="project",
    )(attended, weights.reshape(3 * NY * HD, 6 * HD))
    return projected[None]


def solution(mesh):
    in_specs = (
        P("pass", "seq", "head"),
        P("pass", "seq", "head"),
        P("pass", "seq", "head"),
        P(),
        P(),
        P(),
        P("head", None),
    )
    out_specs = P("pass", "seq", "head")
    return jax.shard_map(
        on_device, mesh=mesh, in_specs=in_specs, out_specs=out_specs, check_vma=False
    )
```

```python
import functools
import math

import jax
import jax.numpy as jnp
from jax import lax
from jax.experimental import pallas as pl
from jax.experimental.pallas import tpu as pltpu
from jax.sharding import PartitionSpec as P

HD = 128
TILE = 128
NX = 4
NZ = 8
NY = 4
SLOTS = 4
ENTRIES = 2 * NZ
BF16 = jnp.bfloat16
F32 = jnp.float32
I32 = jnp.int32
EXP2_SCALE = HD ** -0.5 * math.log2(math.e)
NOTHING = -1e30
MESH = pl.DeviceIdType.MESH


def head_of_row(z):
    return (3 * z + 1) // 8


def first_row(g):
    return (8 * g + 1) // 3


def last_row(g):
    return (8 * g + 9) // 3 - 1


def query_place(zq, g):
    if g == 0:
        return zq // 3, zq % 3
    if g == 1:
        return 3 + zq // 4, zq % 4
    return 7 - (7 - zq) // 3, (7 - zq) % 3


def slot_row(z, g, j):
    low = 3 * z + j
    mid = 4 * (z - 3) + j
    high = 7 - (3 * (7 - z) + j)
    row = jnp.where(g == 0, low, jnp.where(g == 1, mid, high))
    return jnp.where((j == 3) & (g != 1), -1, row)


def row_order(i, z):
    near = jnp.minimum(z, 7 - z)
    d = (i + 1) // 2
    both = z + d * (1 - 2 * (i % 2))
    return jnp.where(i <= 2 * near, both, jnp.where(z <= 3, i, 7 - i))


def remote(src, dst, send, recv, target):
    return pltpu.make_async_remote_copy(
        src_ref=src, dst_ref=dst, send_sem=send, recv_sem=recv, device_id=target, device_id_type=MESH
    )


def greet(devices):
    barrier = pltpu.get_barrier_semaphore()
    for device in devices:
        pl.semaphore_signal(barrier, inc=1, device_id=device, device_id_type=MESH)
    return lambda: pl.semaphore_wait(barrier, len(devices))


def gather_kernel(
    counts_ref, q_ref, k_ref, v_ref, sp_ref, mp_ref, w_ref,
    kv_ref, qs_ref, list_ref, w2_ref,
    mine, list_v,
    z_send, z_recv, zf_send, c_send, c_recv,
    q_send, q_recv, qx_send, qx_recv, w_send, w_recv, wc_send, wc_recv, local_sem,
):
    s = lax.axis_index("seq")
    p = lax.axis_index("pass")
    h = lax.axis_index("head")
    x, z = s // NZ, s % NZ
    zh, y = h // NY, h % NY
    g = head_of_row(z)
    a, b = first_row(g), last_row(g)

    def dev(seq=s, core=p, head=h):
        return {"seq": seq, "pass": core, "head": head}

    def along_x(d):
        return dev(seq=((x + d) % NX) * NZ + z)

    def along_y(d):
        return dev(head=zh * NY + (y + d) % NY)

    met = greet(
        [dev(seq=x * NZ + (z + d) % NZ) for d in range(1, NZ)]
        + [along_x(d) for d in range(1, NX)]
        + [along_y(d) for d in range(1, NY)]
        + [dev(core=1 - p)]
    )

    for n in range(3):
        cols = slice(n * HD, (n + 1) * HD)
        mine[n, :TILE, :] = k_ref[:, cols]
        mine[n, TILE:, :] = v_ref[:, cols].T
    own_copy = pltpu.make_async_copy(mine.at[g], kv_ref.at[z], local_sem.at[0])
    own_copy.start()

    met()

    def query_copies(n):
        row, slot = query_place(z, n)
        src, dst = q_ref.at[:, n * HD:(n + 1) * HD], qs_ref.at[x * SLOTS + slot]
        away = remote(src, dst, q_send.at[n], q_recv.at[slot], dev(seq=x * NZ + row))
        here = pltpu.make_async_copy(src, dst, q_send.at[n])
        return row, away, here

    for n in range(3):
        row, away, here = query_copies(n)
        pl.when(row != z)(away.start)
        pl.when(row == z)(here.start)

    def up_copy(r, src, send):
        return remote(src, kv_ref.at[r], send, z_recv.at[r], dev(seq=s + 1))

    def down_copy(r, src, send):
        return remote(src, kv_ref.at[r], send, z_recv.at[r], dev(seq=s - 1))

    def entry_copy(n):
        e = jnp.maximum(first_row(n), jnp.minimum(z, last_row(n)))
        return e, remote(mine.at[n], kv_ref.at[z], z_send.at[n], z_recv.at[z], dev(seq=x * NZ + e))

    pl.when(z < b)(up_copy(z, mine.at[g], z_send.at[3]).start)
    pl.when(z > a)(down_copy(z, mine.at[g], z_send.at[4]).start)
    for n in range(3):
        e, copy = entry_copy(n)
        pl.when(e != z)(copy.start)

    half_rows = 3 * HD // 2
    rows_mine = pl.ds(pl.multiple_of(p * half_rows, half_rows), half_rows)
    rows_other = pl.ds(pl.multiple_of((1 - p) * half_rows, half_rows), half_rows)

    def w_cols(yy, part):
        zz = zh if part == 0 else 1 - zh
        return pl.ds(pl.multiple_of((zz * NY + yy) * (3 * HD), 3 * HD), 3 * HD)

    def part_cols(part):
        return slice(part * 3 * HD, (part + 1) * 3 * HD)

    def w_copy(d, part):
        return remote(
            w_ref.at[rows_mine, w_cols((y + d) % NY, part)], w2_ref.at[y, rows_mine, part_cols(part)],
            w_send.at[2 * d + part], w_recv.at[2 * d + part], along_y(d),
        )

    def w_arrival(d, part):
        place = w2_ref.at[(y + NY - d) % NY, rows_mine, part_cols(part)]
        return remote(place, place, w_send.at[2 * d + part], w_recv.at[2 * d + part], along_y(d))

    def w_swap(d, rows):
        place = w2_ref.at[(y + NY - d) % NY, rows]
        return remote(place, place, wc_send.at[d], wc_recv.at[d], dev(core=1 - p))

    def w_local(part):
        return pltpu.make_async_copy(
            w_ref.at[:, w_cols(y, part)], w2_ref.at[y, :, part_cols(part)], local_sem.at[1 + part]
        )

    for part in range(2):
        for d in range(1, NY):
            w_copy(d, part).start()
        w_local(part).start()

    slots = lax.broadcasted_iota(I32, (NX * SLOTS, 1), 0)
    tiles = jnp.full((NX * SLOTS, 1), -1, I32)
    for j in range(SLOTS):
        row = slot_row(z, g, j)
        live = (row >= 0) & (row < NZ)
        tiles = jnp.where(((slots & 3) == j) & live, (slots >> 2) * NZ + row, tiles)

    def hits(queries, keys, live_count, shift):
        live = lax.broadcasted_iota(I32, queries.shape, 1) < live_count
        row_hits = ((queries == tiles) & live).astype(F32)
        row = keys - x * NZ
        row = jnp.where((row >= 0) & (row < NZ), row + shift, -1)
        col_hits = (lax.broadcasted_iota(I32, (128, 1), 0) == row).astype(F32)
        return lax.dot_general(row_hits, col_hits, (((1,), (1,)), ((), ())), preferred_element_type=F32)

    is_edit = (p == 1).astype(F32)
    total = hits(sp_ref[p, 0:1], sp_ref[p, 1:2], counts_ref[p], 0)
    total = total + is_edit * hits(mp_ref[0:1], mp_ref[1:2], counts_ref[2], NZ)
    allowed = (total > 0.5).astype(F32)
    earlier = lax.broadcasted_iota(I32, (128, 128), 0) < lax.broadcasted_iota(I32, (128, 128), 1)
    rank = jnp.dot(allowed, earlier.astype(F32), preferred_element_type=F32)
    lanes = lax.broadcasted_iota(I32, (NX * SLOTS, 128), 1)
    picked = allowed * lanes.astype(F32)
    listing = jnp.where(lanes == 127, jnp.sum(allowed, axis=1, keepdims=True), 0.0)
    for at in range(ENTRIES):
        found = jnp.sum(jnp.where(rank == at, picked, 0.0), axis=1, keepdims=True)
        listing = jnp.where(lanes == at, found, listing)
    list_v[...] = listing.astype(I32)
    list_copy = pltpu.make_async_copy(list_v, list_ref, local_sem.at[3])
    list_copy.start()

    def chip_copy(r):
        return remote(kv_ref.at[r], kv_ref.at[NZ + r], c_send.at[r], c_recv.at[r], dev(core=1 - p))

    own_copy.wait()
    pl.when(p == 0)(chip_copy(z).start)

    def pass_on(i, carry):
        r = row_order(i, z)
        place = kv_ref.at[r]
        remote(place, place, z_send.at[0], z_recv.at[r], dev()).wait_recv()
        pl.when((r < z) & (z < b))(up_copy(r, place, zf_send.at[r]).start)
        pl.when((r > z) & (z > a))(down_copy(r, place, zf_send.at[r]).start)
        pl.when(p == 0)(chip_copy(r).start)
        return carry

    lax.fori_loop(1, 3, pass_on, 0)

    def qx_copy(j, d):
        place = qs_ref.at[x * SLOTS + j]
        return remote(place, place, qx_send.at[3 * j + d - 1], qx_recv.at[3 * j + d - 1], along_x(d))

    def qx_arrival(j, d):
        place = qs_ref.at[((x + NX - d) % NX) * SLOTS + j]
        return remote(place, place, qx_send.at[3 * j + d - 1], qx_recv.at[3 * j + d - 1], along_x(d))

    def live_slot(j):
        row = slot_row(z, g, j)
        return row, (row >= 0) & (row < NZ)

    for n in range(3):
        row, away, here = query_copies(n)
        pl.when(row == z)(here.wait)

    for j in range(SLOTS):
        row, live = live_slot(j)
        place = qs_ref.at[x * SLOTS + j]

        @pl.when(live)
        def _():
            pl.when(row != z)(remote(place, place, q_send.at[0], q_recv.at[j], dev()).wait_recv)
            for d in range(1, NX):
                qx_copy(j, d).start()

    lax.fori_loop(3, NZ, pass_on, 0)

    for d in range(1, NY):
        for part in range(2):
            w_arrival(d, part).wait_recv()
        w_swap(d, rows_mine).start()

    def drain(r, carry):
        place = kv_ref.at[r]
        pl.when((r < z) & (z < b))(up_copy(r, place, zf_send.at[r]).wait_send)
        pl.when((r > z) & (z > a))(down_copy(r, place, zf_send.at[r]).wait_send)
        pl.when(p == 0)(chip_copy(r).wait_send)
        pl.when(p == 1)(chip_copy(r).wait_recv)
        return carry

    lax.fori_loop(0, NZ, drain, 0)
    pl.when(z < b)(up_copy(z, mine.at[g], z_send.at[3]).wait_send)
    pl.when(z > a)(down_copy(z, mine.at[g], z_send.at[4]).wait_send)
    for n in range(3):
        e, copy = entry_copy(n)
        pl.when(e != z)(copy.wait_send)
        row, away, here = query_copies(n)
        pl.when(row != z)(away.wait_send)

    for j in range(SLOTS):
        row, live = live_slot(j)

        @pl.when(live)
        def _():
            for d in range(1, NX):
                qx_copy(j, d).wait_send()
                qx_arrival(j, d).wait_recv()

    list_copy.wait()
    for part in range(2):
        w_local(part).wait()
    for d in range(1, NY):
        for part in range(2):
            w_copy(d, part).wait_send()
        w_swap(d, rows_mine).wait_send()
        w_swap(d, rows_other).wait_recv()


def attention_kernel(list_ref, q_ref, kv_ref, o_ref, stat_ref):
    stat_ref[...] = jnp.full(stat_ref.shape, NOTHING, F32)

    def slot(j, carry):
        n = list_ref[j, 127]

        @pl.when(n == 0)
        def _():
            o_ref[j] = jnp.zeros((HD, TILE), BF16)

        @pl.when(n > 0)
        def _():
            query = q_ref[j].T

            def two_tiles(i, state):
                top, total, acc = state
                t, u = list_ref[j, 2 * i], list_ref[j, 2 * i + 1]
                keys = jnp.concatenate([kv_ref[t, :TILE, :], kv_ref[u, :TILE, :]], axis=0)
                values = jnp.concatenate([kv_ref[t, TILE:, :], kv_ref[u, TILE:, :]], axis=1)
                scores = jnp.dot(keys, query, preferred_element_type=F32) * EXP2_SCALE
                second = jnp.where(2 * i + 1 < n, scores[TILE:], NOTHING)
                scores = jnp.concatenate([scores[:TILE], second], axis=0)
                new_top = jnp.maximum(top, jnp.max(scores, axis=0, keepdims=True))
                faded = jnp.exp2(top - new_top)
                exps = jnp.exp2(scores - new_top)
                total = total * faded + jnp.sum(exps.reshape(32, 8, TILE), axis=0)
                acc = acc * faded + jnp.dot(values, exps.astype(BF16), preferred_element_type=F32)
                return new_top, total, acc

            top, total, acc = lax.fori_loop(
                0, (n + 1) // 2, two_tiles,
                (jnp.full((1, TILE), NOTHING, F32), jnp.zeros((8, TILE), F32), jnp.zeros((HD, TILE), F32)),
            )
            row_total = jnp.sum(total, axis=0, keepdims=True)
            o_ref[j] = (acc / row_total).astype(BF16)
            stat_ref[j // SLOTS, pl.ds(j % SLOTS, 1), :] = top + jnp.log2(row_total)

        return carry

    lax.fori_loop(0, NX * SLOTS, slot, 0)


def project_kernel(
    o_ref, stat_ref, w2_ref, out_ref,
    w_v, parts, part_stats, merged, full, give, got,
    x_send, x_recv, s_send, s_recv, o_send, o_recv, y_send, y_recv, h_send, h_recv, local_sem,
):
    s = lax.axis_index("seq")
    p = lax.axis_index("pass")
    h = lax.axis_index("head")
    x, z = s // NZ, s % NZ
    zh, y = h // NY, h % NY
    g = head_of_row(z)

    def dev(seq=s, head=h):
        return {"seq": seq, "pass": p, "head": head}

    def along_x(d):
        return dev(seq=((x + d) % NX) * NZ + z)

    def along_y(d):
        return dev(head=zh * NY + (y + d) % NY)

    partner = dev(head=(1 - zh) * NY + y)
    met = greet(
        [dev(seq=x * NZ + (z + d) % NZ) for d in range(1, NZ)]
        + [along_x(d) for d in range(1, NX)]
        + [along_y(d) for d in range(1, NY)]
        + [partner]
    )
    w_copy = pltpu.make_async_copy(w2_ref, w_v, local_sem.at[0])
    w_copy.start()
    met()

    def live_slot(j):
        row = slot_row(z, g, j)
        return row, (row >= 0) & (row < NZ)

    def stat_copy(d):
        return remote(
            stat_ref.at[(x + d) % NX], part_stats.at[d - 1], s_send.at[d - 1], s_recv.at[d - 1], along_x(d)
        )

    def part_copy(j, d):
        at = 3 * j + d - 1
        return remote(
            o_ref.at[((x + d) % NX) * SLOTS + j], parts.at[at], x_send.at[at], x_recv.at[at], along_x(d)
        )

    for d in range(1, NX):
        stat_copy(d).start()
    for j in range(SLOTS):
        row, live = live_slot(j)

        @pl.when(live)
        def _():
            for d in range(1, NX):
                part_copy(j, d).start()

    def back(j):
        row, live = live_slot(j)
        dst = full.at[3 * y + g]
        away = remote(merged.at[j], dst, o_send.at[j], o_recv.at[g], dev(seq=x * NZ + row))
        here = pltpu.make_async_copy(merged.at[j], dst, o_send.at[j])
        return row, live, away, here

    for d in range(1, NX):
        stat_copy(d).wait_recv()
    for j in range(SLOTS):
        row, live, away, here = back(j)

        @pl.when(live)
        def _():
            stats = [stat_ref[x, j:j + 1, :]] + [part_stats[d, j:j + 1, :] for d in range(3)]
            top = functools.reduce(jnp.maximum, stats)
            shares = [jnp.exp2(stat - top) for stat in stats]
            whole = sum(shares)
            for d in range(1, NX):
                part_copy(j, d).wait_recv()
            blocks = [o_ref[x * SLOTS + j]] + [parts[3 * j + d] for d in range(3)]
            mixed = sum(block.astype(F32) * (share / whole) for block, share in zip(blocks, shares))
            merged[j] = mixed.T.astype(BF16)
            pl.when(row != z)(away.start)
            pl.when(row == z)(here.start)

    def y_copy(n, d):
        block = full.at[3 * y + n]
        return remote(block, block, y_send.at[3 * n + d - 1], y_recv.at[3 * n + d - 1], along_y(d))

    def y_arrival(n, d):
        block = full.at[3 * ((y + NY - d) % NY) + n]
        return remote(block, block, y_send.at[3 * n + d - 1], y_recv.at[3 * n + d - 1], along_y(d))

    for j in range(SLOTS):
        row, live, away, here = back(j)
        pl.when(live & (row == z))(here.wait)

    for n in range(3):
        row, _slot = query_place(z, n)
        block = full.at[3 * y + n]
        pl.when(row != z)(remote(block, block, o_send.at[0], o_recv.at[n], dev()).wait_recv)
        for d in range(1, NY):
            y_copy(n, d).start()

    w_copy.wait()
    for n in range(3):
        for d in range(1, NY):
            y_arrival(n, d).wait_recv()

    def projected(part):
        acc = jnp.zeros((TILE, 3 * HD), F32)
        for n in range(3 * NY):
            acc = acc + jnp.dot(
                full[n], w_v[n * HD:(n + 1) * HD, part * 3 * HD:(part + 1) * 3 * HD],
                preferred_element_type=F32,
            )
        return acc

    give[...] = projected(1).astype(BF16)
    swap = remote(give, got, h_send, h_recv, partner)
    swap.start()
    own = projected(0)
    swap.wait_recv()
    out_ref[...] = (own + got[...].astype(F32)).astype(BF16)

    swap.wait_send()
    for d in range(1, NX):
        stat_copy(d).wait_send()
    for j in range(SLOTS):
        row, live, away, here = back(j)

        @pl.when(live)
        def _():
            for d in range(1, NX):
                part_copy(j, d).wait_send()
            pl.when(row != z)(away.wait_send)

    for n in range(3):
        for d in range(1, NY):
            y_copy(n, d).wait_send()


def on_device(queries, keys, values, self_pairs, mask_pairs, counts, out_weight):
    vmem = pl.BlockSpec(memory_space=pltpu.VMEM)
    smem = pl.BlockSpec(memory_space=pltpu.SMEM)
    hbm = pl.BlockSpec(memory_space=pl.ANY)
    dma = pltpu.SemaphoreType.DMA
    shape = jax.ShapeDtypeStruct
    big = 32 * 1024 * 1024

    tiles, slots, listing, weights = pl.pallas_call(
        gather_kernel,
        out_shape=(
            shape((ENTRIES, 2 * TILE, HD), BF16),
            shape((NX * SLOTS, TILE, HD), BF16),
            shape((NX * SLOTS, 128), I32),
            shape((NY, 3 * HD, 6 * HD), BF16),
        ),
        in_specs=[smem, vmem, vmem, vmem, vmem, vmem, hbm],
        out_specs=(hbm, hbm, hbm, hbm),
        scratch_shapes=[
            pltpu.VMEM((3, 2 * TILE, HD), BF16),
            pltpu.VMEM((NX * SLOTS, 128), I32),
            dma((5,)), dma((NZ,)), dma((NZ,)), dma((NZ,)), dma((NZ,)),
            dma((3,)), dma((SLOTS,)), dma((3 * SLOTS,)), dma((3 * SLOTS,)),
            dma((2 * NY,)), dma((2 * NY,)), dma((NY,)), dma((NY,)), dma((4,)),
        ],
        compiler_params=pltpu.CompilerParams(collective_id=0, has_side_effects=True),
        name="gather_tiles",
    )(
        counts, queries[0], keys[0], values[0],
        jnp.swapaxes(self_pairs, 1, 2), jnp.swapaxes(mask_pairs, 0, 1), out_weight,
    )

    attended, stats = pl.pallas_call(
        attention_kernel,
        out_shape=(shape((NX * SLOTS, HD, TILE), BF16), shape((NX, 8, TILE), F32)),
        in_specs=[smem, vmem, vmem],
        out_specs=(vmem, vmem),
        compiler_params=pltpu.CompilerParams(vmem_limit_bytes=big),
        name="attention",
    )(listing, slots, tiles)

    projected = pl.pallas_call(
        project_kernel,
        out_shape=shape((TILE, 3 * HD), BF16),
        in_specs=[vmem, vmem, hbm],
        out_specs=vmem,
        scratch_shapes=[
            pltpu.VMEM((3 * NY * HD, 6 * HD), BF16),
            pltpu.VMEM((3 * SLOTS, HD, TILE), BF16),
            pltpu.VMEM((3, 8, TILE), F32),
            pltpu.VMEM((SLOTS, TILE, HD), BF16),
            pltpu.VMEM((3 * NY, TILE, HD), BF16),
            pltpu.VMEM((TILE, 3 * HD), BF16),
            pltpu.VMEM((TILE, 3 * HD), BF16),
            dma((3 * SLOTS,)), dma((3 * SLOTS,)), dma((3,)), dma((3,)),
            dma((SLOTS,)), dma((3,)), dma((9,)), dma((9,)), dma, dma, dma((1,)),
        ],
        compiler_params=pltpu.CompilerParams(collective_id=1, has_side_effects=True, vmem_limit_bytes=big),
        name="project",
    )(attended, stats, weights.reshape(3 * NY * HD, 6 * HD))
    return projected[None]


def solution(mesh):
    in_specs = (
        P("pass", "seq", "head"),
        P("pass", "seq", "head"),
        P("pass", "seq", "head"),
        P(),
        P(),
        P(),
        P("head", None),
    )
    out_specs = P("pass", "seq", "head")
    return jax.shard_map(
        on_device, mesh=mesh, in_specs=in_specs, out_specs=out_specs, check_vma=False
    )
```

```python
import functools
import math

import jax
import jax.numpy as jnp
from jax import lax
from jax.experimental import pallas as pl
from jax.experimental.pallas import tpu as pltpu
from jax.sharding import PartitionSpec as P

HD = 128
TILE = 128
NX = 4
NZ = 8
NY = 4
SLOTS = 4
ENTRIES = 2 * NZ
BF16 = jnp.bfloat16
F32 = jnp.float32
I32 = jnp.int32
EXP2_SCALE = HD ** -0.5 * math.log2(math.e)
NOTHING = -1e30
QUERIES = NX * SLOTS * TILE
MESH = pl.DeviceIdType.MESH


def head_of_row(z):
    return (3 * z + 1) // 8


def first_row(g):
    return (8 * g + 1) // 3


def last_row(g):
    return (8 * g + 9) // 3 - 1


def query_place(zq, g):
    if g == 0:
        return zq // 3, zq % 3
    if g == 1:
        return 3 + zq // 4, zq % 4
    return 7 - (7 - zq) // 3, (7 - zq) % 3


def slot_row(z, g, j):
    low = 3 * z + j
    mid = 4 * (z - 3) + j
    high = 7 - (3 * (7 - z) + j)
    row = jnp.where(g == 0, low, jnp.where(g == 1, mid, high))
    return jnp.where((j == 3) & (g != 1), -1, row)


def row_order(i, z):
    near = jnp.minimum(z, 7 - z)
    d = (i + 1) // 2
    both = z + d * (1 - 2 * (i % 2))
    return jnp.where(i <= 2 * near, both, jnp.where(z <= 3, i, 7 - i))


def remote(src, dst, send, recv, target):
    return pltpu.make_async_remote_copy(
        src_ref=src, dst_ref=dst, send_sem=send, recv_sem=recv, device_id=target, device_id_type=MESH
    )


def layer_kernel(
    counts_ref, q_ref, k_ref, v_ref, sp_ref, mp_ref, w_ref, out_ref,
    q_v, k_v, v_v, sp_v, mp_v, counts_v,
    mine, kv, qs, qt, bias, tops, totals, acc, w_v,
    o_v, stat_v, parts, part_stats, merged, full, give, got,
    z_send, z_recv, zf_send, c_send, c_recv,
    q_send, q_recv, qx_send, qx_recv, w_send, w_recv, wc_send, wc_recv,
    x_send, x_recv, s_send, s_recv, o_send, o_recv, y_send, y_recv, h_send, h_recv, local_sem,
):
    s = lax.axis_index("seq")
    p = lax.axis_index("pass")
    h = lax.axis_index("head")
    x, z = s // NZ, s % NZ
    zh, y = h // NY, h % NY
    g = head_of_row(z)
    a, b = first_row(g), last_row(g)

    def dev(seq=s, core=p, head=h):
        return {"seq": seq, "pass": core, "head": head}

    def along_x(d):
        return dev(seq=((x + d) % NX) * NZ + z)

    def along_y(d):
        return dev(head=zh * NY + (y + d) % NY)

    partner = dev(head=(1 - zh) * NY + y)
    met = (
        [dev(seq=x * NZ + (z + d) % NZ) for d in range(1, NZ)]
        + [along_x(d) for d in range(1, NX)]
        + [along_y(d) for d in range(1, NY)]
        + [dev(core=1 - p), partner]
    )
    barrier = pltpu.get_barrier_semaphore()
    for device in met:
        pl.semaphore_signal(barrier, inc=1, device_id=device, device_id_type=MESH)

    def w_cols(yy, part):
        zz = zh if part == 0 else 1 - zh
        return pl.ds(pl.multiple_of((zz * NY + yy) * (3 * HD), 3 * HD), 3 * HD)

    def part_cols(part):
        return slice(part * 3 * HD, (part + 1) * 3 * HD)

    loads = [
        pltpu.make_async_copy(src, dst, local_sem.at[i])
        for i, (src, dst) in enumerate(
            [(k_ref, k_v), (v_ref, v_v), (q_ref, q_v), (counts_ref, counts_v), (sp_ref, sp_v), (mp_ref, mp_v)]
            + [(w_ref.at[:, w_cols(y, part)], w_v.at[y, :, part_cols(part)]) for part in range(2)]
        )
    ]
    for load in loads:
        load.start()

    loads[0].wait()
    loads[1].wait()
    for n in range(3):
        cols = slice(n * HD, (n + 1) * HD)
        mine[n, :TILE, :] = k_v[:, cols]
        mine[n, TILE:, :] = v_v[:, cols].T
    kv[z] = mine[g]
    loads[2].wait()

    pl.semaphore_wait(barrier, len(met))

    def query_copies(n):
        row, slot = query_place(z, n)
        src, dst = q_v.at[:, n * HD:(n + 1) * HD], qs.at[slot * NX + x]
        away = remote(src, dst, q_send.at[n], q_recv.at[slot], dev(seq=x * NZ + row))
        here = pltpu.make_async_copy(src, dst, q_send.at[n])
        return row, away, here

    for n in range(3):
        row, away, here = query_copies(n)
        pl.when(row != z)(away.start)
        pl.when(row == z)(here.start)

    def up_copy(r, src, send):
        return remote(src, kv.at[r], send, z_recv.at[r], dev(seq=s + 1))

    def down_copy(r, src, send):
        return remote(src, kv.at[r], send, z_recv.at[r], dev(seq=s - 1))

    def entry_copy(n):
        e = jnp.maximum(first_row(n), jnp.minimum(z, last_row(n)))
        return e, remote(mine.at[n], kv.at[z], z_send.at[n], z_recv.at[z], dev(seq=x * NZ + e))

    pl.when(z < b)(up_copy(z, mine.at[g], z_send.at[3]).start)
    pl.when(z > a)(down_copy(z, mine.at[g], z_send.at[4]).start)
    for n, far in ((1, None), (0, z >= first_row(2)), (2, z <= last_row(0))):
        e, copy = entry_copy(n)
        pl.when((e != z) if far is None else (e != z) & jnp.logical_not(far))(copy.start)

    half_rows = 3 * HD // 2
    rows_mine = pl.ds(pl.multiple_of(p * half_rows, half_rows), half_rows)
    rows_other = pl.ds(pl.multiple_of((1 - p) * half_rows, half_rows), half_rows)

    def w_copy(d, part):
        return remote(
            w_ref.at[rows_mine, w_cols((y + d) % NY, part)], w_v.at[y, rows_mine, part_cols(part)],
            w_send.at[2 * d + part], w_recv.at[2 * d + part], along_y(d),
        )

    def w_arrival(d, part):
        place = w_v.at[(y + NY - d) % NY, rows_mine, part_cols(part)]
        return remote(place, place, w_send.at[2 * d + part], w_recv.at[2 * d + part], along_y(d))

    def w_swap(d, rows):
        place = w_v.at[(y + NY - d) % NY, rows]
        return remote(place, place, wc_send.at[d], wc_recv.at[d], dev(core=1 - p))

    for part in range(2):
        for d in range(1, NY):
            w_copy(d, part).start()

    for load in loads[3:6]:
        load.wait()
    slots = lax.broadcasted_iota(I32, (NX * SLOTS, 1), 0)
    tiles = jnp.full((NX * SLOTS, 1), -1, I32)
    for j in range(SLOTS):
        row = slot_row(z, g, j)
        live = (row >= 0) & (row < NZ)
        tiles = jnp.where(((slots >> 2) == j) & live, (slots & 3) * NZ + row, tiles)

    def hits(queries, keys, live_count, shift):
        live = lax.broadcasted_iota(I32, queries.shape, 1) < live_count
        row_hits = ((queries == tiles) & live).astype(F32)
        row = keys - x * NZ
        row = jnp.where((row >= 0) & (row < NZ), row + shift, -1)
        col_hits = (lax.broadcasted_iota(I32, (ENTRIES, 1), 0) == row).astype(F32)
        return lax.dot_general(col_hits, row_hits, (((1,), (1,)), ((), ())), preferred_element_type=F32)

    is_edit = (p == 1).astype(F32)
    counted = hits(sp_v[p, 0:1], sp_v[p, 1:2], counts_v[p], 0)
    counted = counted + is_edit * hits(mp_v[0:1], mp_v[1:2], counts_v[2], NZ)
    allowed = (counted > 0.5).astype(F32)
    spread = lax.broadcasted_iota(I32, (NX * SLOTS, QUERIES), 1) // TILE
    spread = (spread == lax.broadcasted_iota(I32, (NX * SLOTS, QUERIES), 0)).astype(F32)
    live = jnp.dot(allowed, spread, preferred_element_type=F32)
    bias[...] = jnp.where(live > 0.5, 0.0, NOTHING)
    tops[...] = jnp.full(tops.shape, NOTHING, F32)
    totals[...] = jnp.zeros(totals.shape, F32)
    acc[...] = jnp.zeros(acc.shape, F32)

    def chip_copy(r):
        return remote(kv.at[r], kv.at[NZ + r], c_send.at[r], c_recv.at[r], dev(core=1 - p))

    pl.when(p == 0)(chip_copy(z).start)

    def pass_on(i):
        r = row_order(i, z)
        place = kv.at[r]
        remote(place, place, z_send.at[0], z_recv.at[r], dev()).wait_recv()
        pl.when((r < z) & (z < b))(up_copy(r, place, zf_send.at[r]).start)
        pl.when((r > z) & (z > a))(down_copy(r, place, zf_send.at[r]).start)
        pl.when(p == 0)(chip_copy(r).start)

    def qx_copy(j, d):
        place = qs.at[j * NX + x]
        return remote(place, place, qx_send.at[3 * j + d - 1], qx_recv.at[3 * j + d - 1], along_x(d))

    def qx_arrival(j, d):
        place = qs.at[j * NX + (x + NX - d) % NX]
        return remote(place, place, qx_send.at[3 * j + d - 1], qx_recv.at[3 * j + d - 1], along_x(d))

    def live_slot(j):
        row = slot_row(z, g, j)
        return row, (row >= 0) & (row < NZ)

    for n in range(3):
        row, away, here = query_copies(n)
        pl.when(row == z)(here.wait)

    for j in range(SLOTS):
        row, live = live_slot(j)
        place = qs.at[j * NX + x]

        @pl.when(live)
        def _():
            pl.when(row != z)(remote(place, place, q_send.at[0], q_recv.at[j], dev()).wait_recv)
            for d in range(1, NX):
                qx_copy(j, d).start()

    pass_on(1)

    for n, near, far in ((0, 1, z >= first_row(2)), (2, 1, z <= last_row(0))):
        @pl.when(far)
        def _():
            entry_copy(near)[1].wait_send()
            entry_copy(n)[1].start()

    pass_on(2)

    for j in range(SLOTS):
        row, live = live_slot(j)

        @pl.when(live)
        def _():
            for d in range(1, NX):
                qx_arrival(j, d).wait_recv()
            for xx in range(NX):
                at = j * NX + xx
                qt[:, at * TILE:(at + 1) * TILE] = qs[at].T

    def attend(r, u, base):
        keys = jnp.concatenate([kv[base + r, :TILE, :], kv[base + u, :TILE, :]], axis=0)
        values = jnp.concatenate([kv[base + r, TILE:, :], kv[base + u, TILE:, :]], axis=1)

        def unit(i, carry):
            row, live = live_slot(i // 2)

            @pl.when(live)
            def _():
                cols = pl.ds(pl.multiple_of(i * 2 * TILE, 2 * TILE), 2 * TILE)
                scores = jnp.dot(keys, qt[:, cols], preferred_element_type=F32)
                first, second = scores[:TILE], scores[TILE:]
                first_bias = bias[pl.ds(base + r, 1), cols]
                second_bias = bias[pl.ds(base + u, 1), cols]
                top = tops[:, cols]
                new_top = jnp.maximum(top, jnp.maximum(
                    jnp.max(first, axis=0, keepdims=True) * EXP2_SCALE + first_bias,
                    jnp.max(second, axis=0, keepdims=True) * EXP2_SCALE + second_bias,
                ))
                level = jnp.maximum(new_top, NOTHING / 10)
                faded = jnp.exp2(top - new_top)
                first = jnp.exp2(first * EXP2_SCALE - (level - first_bias))
                second = jnp.exp2(second * EXP2_SCALE - (level - second_bias))
                tops[:, cols] = new_top
                totals[:, cols] = totals[:, cols] * faded + jnp.sum(
                    (first + second).reshape(16, 8, 2 * TILE), axis=0
                )
                weights = jnp.concatenate([first.astype(BF16), second.astype(BF16)], axis=0)
                acc[:, cols] = acc[:, cols] * faded + jnp.dot(values, weights, preferred_element_type=F32)

            return carry

        lax.fori_loop(0, 2 * SLOTS, unit, 0)

    def batch(i, carry):
        r, u = row_order(2 * i, z), row_order(2 * i + 1, z)

        @pl.when(i > 0)
        def _():
            pl.when(i > 1)(lambda: pass_on(2 * i))
            pass_on(2 * i + 1)

        attend(r, u, 0)

        @pl.when(p == 1)
        def _():
            chip_copy(r).wait_recv()
            chip_copy(u).wait_recv()
            attend(r, u, NZ)

        return carry

    lax.fori_loop(0, NZ // 2, batch, 0)

    whole = jnp.sum(totals[...], axis=0, keepdims=True)
    some = whole > 0.0
    inverse = 1.0 / jnp.where(some, whole, 1.0)
    level = jnp.where(some, tops[...] + jnp.log2(jnp.where(some, whole, 1.0)), NOTHING)
    for j in range(SLOTS):
        for xx in range(NX):
            at = j * NX + xx
            cols = slice(at * TILE, (at + 1) * TILE)
            stat_v[xx, j:j + 1, :] = level[:, cols]

    def stat_copy(d):
        return remote(
            stat_v.at[(x + d) % NX], part_stats.at[d - 1], s_send.at[d - 1], s_recv.at[d - 1], along_x(d)
        )

    def part_copy(j, d):
        at = 3 * j + d - 1
        return remote(
            o_v.at[j * NX + (x + d) % NX], parts.at[at], x_send.at[at], x_recv.at[at], along_x(d)
        )

    for d in range(1, NX):
        stat_copy(d).start()
    for j in range(SLOTS):
        row, live = live_slot(j)

        @pl.when(live)
        def _():
            for xx in range(NX):
                at = j * NX + xx
                cols = slice(at * TILE, (at + 1) * TILE)
                o_v[at] = (acc[:, cols] * inverse[:, cols]).astype(BF16)
            for d in range(1, NX):
                part_copy(j, d).start()

    for d in range(1, NY):
        for part in range(2):
            w_arrival(d, part).wait_recv()
        w_swap(d, rows_mine).start()

    def back(j):
        row, live = live_slot(j)
        dst = full.at[3 * y + g]
        away = remote(merged.at[j], dst, o_send.at[j], o_recv.at[g], dev(seq=x * NZ + row))
        here = pltpu.make_async_copy(merged.at[j], dst, o_send.at[j])
        return row, live, away, here

    for d in range(1, NX):
        stat_copy(d).wait_recv()
    for j in range(SLOTS):
        row, live, away, here = back(j)

        @pl.when(live)
        def _():
            stats = [stat_v[x, j:j + 1, :]] + [part_stats[d, j:j + 1, :] for d in range(3)]
            top = functools.reduce(jnp.maximum, stats)
            shares = [jnp.exp2(stat - top) for stat in stats]
            share_sum = sum(shares)
            for d in range(1, NX):
                part_copy(j, d).wait_recv()
            blocks = [o_v[j * NX + x]] + [parts[3 * j + d] for d in range(3)]
            mixed = sum(block.astype(F32) * (share / share_sum) for block, share in zip(blocks, shares))
            merged[j] = mixed.T.astype(BF16)
            pl.when(row != z)(away.start)
            pl.when(row == z)(here.start)

    def y_copy(n, d):
        block = full.at[3 * y + n]
        return remote(block, block, y_send.at[3 * n + d - 1], y_recv.at[3 * n + d - 1], along_y(d))

    def y_arrival(n, d):
        block = full.at[3 * ((y + NY - d) % NY) + n]
        return remote(block, block, y_send.at[3 * n + d - 1], y_recv.at[3 * n + d - 1], along_y(d))

    for j in range(SLOTS):
        row, live, away, here = back(j)
        pl.when(live & (row == z))(here.wait)

    for n in range(3):
        row, _slot = query_place(z, n)
        block = full.at[3 * y + n]
        pl.when(row != z)(remote(block, block, o_send.at[0], o_recv.at[n], dev()).wait_recv)
        for d in range(1, NY):
            y_copy(n, d).start()

    for load in loads[6:]:
        load.wait()
    for d in range(1, NY):
        w_swap(d, rows_other).wait_recv()
    for n in range(3):
        for d in range(1, NY):
            y_arrival(n, d).wait_recv()

    def projected(part):
        total = jnp.zeros((TILE, 3 * HD), F32)
        for n in range(3 * NY):
            weights = w_v[n // 3, n % 3 * HD:(n % 3 + 1) * HD, part_cols(part)]
            total = total + jnp.dot(full[n], weights, preferred_element_type=F32)
        return total

    give[...] = projected(1).astype(BF16)
    swap = remote(give, got, h_send, h_recv, partner)
    swap.start()
    own = projected(0)
    swap.wait_recv()
    out_ref[...] = (own + got[...].astype(F32)).astype(BF16)

    def drain(r, carry):
        place = kv.at[r]
        pl.when((r < z) & (z < b))(up_copy(r, place, zf_send.at[r]).wait_send)
        pl.when((r > z) & (z > a))(down_copy(r, place, zf_send.at[r]).wait_send)
        pl.when(p == 0)(chip_copy(r).wait_send)
        return carry

    lax.fori_loop(0, NZ, drain, 0)
    pl.when(z < b)(up_copy(z, mine.at[g], z_send.at[3]).wait_send)
    pl.when(z > a)(down_copy(z, mine.at[g], z_send.at[4]).wait_send)
    middle = (z > last_row(0)) & (z < first_row(2))
    for n in range(3):
        e, copy = entry_copy(n)
        pl.when(((e != z) & middle) if n == 1 else (e != z))(copy.wait_send)
        row, away, here = query_copies(n)
        pl.when(row != z)(away.wait_send)

    for j in range(SLOTS):
        row, live, away, here = back(j)

        @pl.when(live)
        def _():
            for d in range(1, NX):
                qx_copy(j, d).wait_send()
                part_copy(j, d).wait_send()
            pl.when(row != z)(away.wait_send)

    for d in range(1, NX):
        stat_copy(d).wait_send()
    for d in range(1, NY):
        for part in range(2):
            w_copy(d, part).wait_send()
        w_swap(d, rows_mine).wait_send()
        for n in range(3):
            y_copy(n, d).wait_send()
    swap.wait_send()


def on_device(queries, keys, values, self_pairs, mask_pairs, counts, out_weight):
    hbm = pl.BlockSpec(memory_space=pltpu.HBM)
    vmem = pltpu.VMEM
    dma = pltpu.SemaphoreType.DMA
    rows = (TILE, 3 * HD)
    projected = pl.pallas_call(
        layer_kernel,
        out_shape=jax.ShapeDtypeStruct(rows, BF16),
        in_specs=[hbm] * 7,
        out_specs=pl.BlockSpec(memory_space=vmem),
        scratch_shapes=[
            vmem(rows, BF16), vmem(rows, BF16), vmem(rows, BF16),
            vmem((2, 2, self_pairs.shape[1]), I32), vmem((2, mask_pairs.shape[0]), I32), pltpu.SMEM((3,), I32),
            vmem((3, 2 * TILE, HD), BF16),
            vmem((ENTRIES, 2 * TILE, HD), BF16),
            vmem((NX * SLOTS, TILE, HD), BF16),
            vmem((HD, QUERIES), BF16),
            vmem((ENTRIES, QUERIES), F32),
            vmem((1, QUERIES), F32),
            vmem((8, QUERIES), F32),
            vmem((HD, QUERIES), F32),
            vmem((NY, 3 * HD, 6 * HD), BF16),
            vmem((NX * SLOTS, HD, TILE), BF16),
            vmem((NX, 8, TILE), F32),
            vmem((3 * SLOTS, HD, TILE), BF16),
            vmem((3, 8, TILE), F32),
            vmem((SLOTS, TILE, HD), BF16),
            vmem((3 * NY, TILE, HD), BF16),
            vmem(rows, BF16), vmem(rows, BF16),
            dma((5,)), dma((NZ,)), dma((NZ,)), dma((NZ,)), dma((NZ,)),
            dma((3,)), dma((SLOTS,)), dma((3 * SLOTS,)), dma((3 * SLOTS,)),
            dma((2 * NY,)), dma((2 * NY,)), dma((NY,)), dma((NY,)),
            dma((3 * SLOTS,)), dma((3 * SLOTS,)), dma((3,)), dma((3,)),
            dma((SLOTS,)), dma((3,)), dma((9,)), dma((9,)), dma, dma, dma((8,)),
        ],
        compiler_params=pltpu.CompilerParams(
            collective_id=0, has_side_effects=True, vmem_limit_bytes=60 * 1024 * 1024
        ),
        name="layer",
    )(
        counts, queries[0], keys[0], values[0],
        jnp.swapaxes(self_pairs, 1, 2), jnp.swapaxes(mask_pairs, 0, 1), out_weight,
    )
    return projected[None]


def solution(mesh):
    in_specs = (
        P("pass", "seq", "head"),
        P("pass", "seq", "head"),
        P("pass", "seq", "head"),
        P(),
        P(),
        P(),
        P("head", None),
    )
    out_specs = P("pass", "seq", "head")
    return jax.shard_map(
        on_device, mesh=mesh, in_specs=in_specs, out_specs=out_specs, check_vma=False
    )
```

```python
import functools
import math

import jax
import jax.numpy as jnp
from jax import lax
from jax.experimental import pallas as pl
from jax.experimental.pallas import tpu as pltpu
from jax.sharding import PartitionSpec as P

HD = 128
TILE = 128
NX = 4
NZ = 8
NY = 4
SLOTS = 4
ENTRIES = 2 * NZ
BF16 = jnp.bfloat16
F32 = jnp.float32
I32 = jnp.int32
EXP2_SCALE = HD ** -0.5 * math.log2(math.e)
NOTHING = -1e30
QUERIES = NX * SLOTS * TILE
MESH = pl.DeviceIdType.MESH


def head_of_row(z):
    return (3 * z + 1) // 8


def first_row(g):
    return (8 * g + 1) // 3


def last_row(g):
    return (8 * g + 9) // 3 - 1


def query_place(zq, g):
    if g == 0:
        return zq // 3, zq % 3
    if g == 1:
        return 3 + zq // 4, zq % 4
    return 7 - (7 - zq) // 3, (7 - zq) % 3


def slot_row(z, g, j):
    low = 3 * z + j
    mid = 4 * (z - 3) + j
    high = 7 - (3 * (7 - z) + j)
    row = jnp.where(g == 0, low, jnp.where(g == 1, mid, high))
    return jnp.where((j == 3) & (g != 1), -1, row)


def row_order(i, z):
    near = jnp.minimum(z, 7 - z)
    d = (i + 1) // 2
    both = z + d * (1 - 2 * (i % 2))
    return jnp.where(i <= 2 * near, both, jnp.where(z <= 3, i, 7 - i))


def remote(src, dst, send, recv, target):
    return pltpu.make_async_remote_copy(
        src_ref=src, dst_ref=dst, send_sem=send, recv_sem=recv, device_id=target, device_id_type=MESH
    )


def layer_kernel(
    counts_ref, q_ref, k_ref, v_ref, sp_ref, mp_ref, w_ref, out_ref,
    q_v, k_v, v_v, sp_v, mp_v, counts_v,
    mine, kv, qs, qt, bias, tops, totals, acc, w_v,
    o_v, stat_v, parts, part_stats, merged, full, give, got,
    z_send, z_recv, zf_send, c_send, c_recv,
    q_send, q_recv, qx_send, qx_recv, w_send, w_recv, wc_send, wc_recv,
    x_send, x_recv, s_send, s_recv, o_send, o_recv, y_send, y_recv, h_send, h_recv, turn, local_sem,
):
    s = lax.axis_index("seq")
    p = lax.axis_index("pass")
    h = lax.axis_index("head")
    x, z = s // NZ, s % NZ
    zh, y = h // NY, h % NY
    g = head_of_row(z)
    a, b = first_row(g), last_row(g)

    def dev(seq=s, core=p, head=h):
        return {"seq": seq, "pass": core, "head": head}

    def along_x(d):
        return dev(seq=((x + d) % NX) * NZ + z)

    def along_y(d):
        return dev(head=zh * NY + (y + d) % NY)

    partner = dev(head=(1 - zh) * NY + y)
    met = (
        [dev(seq=x * NZ + (z + d) % NZ) for d in range(1, NZ)]
        + [along_x(d) for d in range(1, NX)]
        + [along_y(d) for d in range(1, NY)]
        + [dev(core=1 - p), partner]
    )
    barrier = pltpu.get_barrier_semaphore()
    for device in met:
        pl.semaphore_signal(barrier, inc=1, device_id=device, device_id_type=MESH)

    def w_cols(yy, part):
        zz = zh if part == 0 else 1 - zh
        return pl.ds(pl.multiple_of((zz * NY + yy) * (3 * HD), 3 * HD), 3 * HD)

    def part_cols(part):
        return slice(part * 3 * HD, (part + 1) * 3 * HD)

    loads = [
        pltpu.make_async_copy(src, dst, local_sem.at[i])
        for i, (src, dst) in enumerate(
            [(k_ref, k_v), (v_ref, v_v), (q_ref, q_v), (counts_ref, counts_v), (sp_ref, sp_v), (mp_ref, mp_v)]
            + [(w_ref.at[:, w_cols(y, part)], w_v.at[y, :, part_cols(part)]) for part in range(2)]
        )
    ]
    for load in loads:
        load.start()

    loads[0].wait()
    loads[1].wait()
    for n in range(3):
        cols = slice(n * HD, (n + 1) * HD)
        mine[n, :TILE, :] = k_v[:, cols]
        mine[n, TILE:, :] = v_v[:, cols].T
    kv[z] = mine[g]
    loads[2].wait()

    pl.semaphore_wait(barrier, len(met))

    def query_copies(n):
        row, slot = query_place(z, n)
        src, dst = q_v.at[:, n * HD:(n + 1) * HD], qs.at[slot * NX + x]
        away = remote(src, dst, q_send.at[n], q_recv.at[slot], dev(seq=x * NZ + row))
        here = pltpu.make_async_copy(src, dst, q_send.at[n])
        return row, away, here

    for n in range(3):
        row, away, here = query_copies(n)
        pl.when(row != z)(away.start)
        pl.when(row == z)(here.start)

    def up_copy(r, src, send):
        return remote(src, kv.at[r], send, z_recv.at[r], dev(seq=s + 1))

    def down_copy(r, src, send):
        return remote(src, kv.at[r], send, z_recv.at[r], dev(seq=s - 1))

    def entry_copy(n):
        e = jnp.maximum(first_row(n), jnp.minimum(z, last_row(n)))
        return e, remote(mine.at[n], kv.at[z], z_send.at[n], z_recv.at[z], dev(seq=x * NZ + e))

    pl.when(z < b)(up_copy(z, mine.at[g], z_send.at[3]).start)
    pl.when(z > a)(down_copy(z, mine.at[g], z_send.at[4]).start)
    def later(e):
        return (p == 1) & ((e - z) * (e - z) > 1)

    for n in range(3):
        e, copy = entry_copy(n)
        pl.when((e != z) & jnp.logical_not(later(e)))(copy.start)

    half_rows = 3 * HD // 2
    rows_mine = pl.ds(pl.multiple_of(p * half_rows, half_rows), half_rows)
    rows_other = pl.ds(pl.multiple_of((1 - p) * half_rows, half_rows), half_rows)

    def w_copy(d, part):
        return remote(
            w_ref.at[rows_mine, w_cols((y + d) % NY, part)], w_v.at[y, rows_mine, part_cols(part)],
            w_send.at[2 * d + part], w_recv.at[2 * d + part], along_y(d),
        )

    def w_arrival(d, part):
        place = w_v.at[(y + NY - d) % NY, rows_mine, part_cols(part)]
        return remote(place, place, w_send.at[2 * d + part], w_recv.at[2 * d + part], along_y(d))

    def w_swap(d, rows):
        place = w_v.at[(y + NY - d) % NY, rows]
        return remote(place, place, wc_send.at[d], wc_recv.at[d], dev(core=1 - p))

    for part in range(2):
        for d in range(1, NY):
            w_copy(d, part).start()

    for load in loads[3:6]:
        load.wait()
    slots = lax.broadcasted_iota(I32, (NX * SLOTS, 1), 0)
    tiles = jnp.full((NX * SLOTS, 1), -1, I32)
    for j in range(SLOTS):
        row = slot_row(z, g, j)
        live = (row >= 0) & (row < NZ)
        tiles = jnp.where(((slots >> 2) == j) & live, (slots & 3) * NZ + row, tiles)

    def hits(queries, keys, live_count, shift):
        live = lax.broadcasted_iota(I32, queries.shape, 1) < live_count
        row_hits = ((queries == tiles) & live).astype(F32)
        row = keys - x * NZ
        row = jnp.where((row >= 0) & (row < NZ), row + shift, -1)
        col_hits = (lax.broadcasted_iota(I32, (ENTRIES, 1), 0) == row).astype(F32)
        return lax.dot_general(col_hits, row_hits, (((1,), (1,)), ((), ())), preferred_element_type=F32)

    is_edit = (p == 1).astype(F32)
    counted = hits(sp_v[p, 0:1], sp_v[p, 1:2], counts_v[p], 0)
    counted = counted + is_edit * hits(mp_v[0:1], mp_v[1:2], counts_v[2], NZ)
    allowed = (counted > 0.5).astype(F32)
    spread = lax.broadcasted_iota(I32, (NX * SLOTS, QUERIES), 1) // TILE
    spread = (spread == lax.broadcasted_iota(I32, (NX * SLOTS, QUERIES), 0)).astype(F32)
    live = jnp.dot(allowed, spread, preferred_element_type=F32)
    bias[...] = jnp.where(live > 0.5, 0.0, NOTHING)
    tops[...] = jnp.full(tops.shape, NOTHING, F32)
    totals[...] = jnp.zeros(totals.shape, F32)
    acc[...] = jnp.zeros(acc.shape, F32)

    def chip_copy(r):
        return remote(kv.at[r], kv.at[NZ + r], c_send.at[r], c_recv.at[r], dev(core=1 - p))

    pl.when(p == 0)(chip_copy(z).start)

    def pass_on(i):
        r = row_order(i, z)
        place = kv.at[r]
        remote(place, place, z_send.at[0], z_recv.at[r], dev()).wait_recv()
        pl.when((r < z) & (z < b))(up_copy(r, place, zf_send.at[r]).start)
        pl.when((r > z) & (z > a))(down_copy(r, place, zf_send.at[r]).start)
        pl.when(p == 0)(chip_copy(r).start)

    def qx_copy(j, d):
        place = qs.at[j * NX + x]
        return remote(place, place, qx_send.at[3 * j + d - 1], qx_recv.at[3 * j + d - 1], along_x(d))

    def qx_arrival(j, d):
        place = qs.at[j * NX + (x + NX - d) % NX]
        return remote(place, place, qx_send.at[3 * j + d - 1], qx_recv.at[3 * j + d - 1], along_x(d))

    def live_slot(j):
        row = slot_row(z, g, j)
        return row, (row >= 0) & (row < NZ)

    for n in range(3):
        row, away, here = query_copies(n)
        pl.when(row == z)(here.wait)

    for j in range(SLOTS):
        row, live = live_slot(j)
        place = qs.at[j * NX + x]

        @pl.when(live)
        def _():
            pl.when(row != z)(remote(place, place, q_send.at[0], q_recv.at[j], dev()).wait_recv)
            for d in range(1, NX):
                qx_copy(j, d).start()

    pass_on(1)

    pass_on(2)

    @pl.when(p == 0)
    def _():
        for n in range(3):
            e, copy = entry_copy(n)
            pl.when(e != z)(copy.wait_send)
        pl.semaphore_signal(turn, inc=1, device_id=dev(core=1), device_id_type=MESH)

        def passing(i, carry):
            pass_on(i)
            return carry

        lax.fori_loop(3, NZ, passing, 0)

    @pl.when(p == 1)
    def _():
        pl.semaphore_wait(turn, 1)
        for n in range(3):
            e, copy = entry_copy(n)
            pl.when(later(e))(copy.start)

    for j in range(SLOTS):
        row, live = live_slot(j)

        @pl.when(live)
        def _():
            for d in range(1, NX):
                qx_arrival(j, d).wait_recv()
            for xx in range(NX):
                at = j * NX + xx
                qt[:, at * TILE:(at + 1) * TILE] = qs[at].T

    live_slots = jnp.where(g == 1, 4, jnp.where((z == 2) | (z == 5), 2, 3))

    def attend(r, u, base):
        for width in range(2, SLOTS + 1):
            pl.when(live_slots == width)(functools.partial(attend_slots, r, u, base, width * NX * TILE))

    def attend_slots(r, u, base, width):
        cols = slice(0, width)
        keys = jnp.concatenate([kv[base + r, :TILE, :], kv[base + u, :TILE, :]], axis=0)
        values = jnp.concatenate([kv[base + r, TILE:, :], kv[base + u, TILE:, :]], axis=1)
        scores = jnp.dot(keys, qt[:, cols], preferred_element_type=F32)
        first, second = scores[:TILE], scores[TILE:]
        first_bias = bias[pl.ds(base + r, 1), cols]
        second_bias = bias[pl.ds(base + u, 1), cols]
        top = tops[:, cols]
        new_top = jnp.maximum(top, jnp.maximum(
            jnp.max(first, axis=0, keepdims=True) * EXP2_SCALE + first_bias,
            jnp.max(second, axis=0, keepdims=True) * EXP2_SCALE + second_bias,
        ))
        level = jnp.maximum(new_top, NOTHING / 10)
        faded = jnp.exp2(top - new_top)
        first = jnp.exp2(first * EXP2_SCALE - (level - first_bias))
        second = jnp.exp2(second * EXP2_SCALE - (level - second_bias))
        tops[:, cols] = new_top
        totals[:, cols] = totals[:, cols] * faded + jnp.sum((first + second).reshape(16, 8, width), axis=0)
        weights = jnp.concatenate([first.astype(BF16), second.astype(BF16)], axis=0)
        acc[:, cols] = acc[:, cols] * faded + jnp.dot(values, weights, preferred_element_type=F32)

    def step(i, carry):
        cross = (i != 1) & (i < 5)
        at = jnp.where(i < 2, 0, jnp.where(i < 5, i - 1, i - 4))
        r, u = row_order(2 * at, z), row_order(2 * at + 1, z)

        @pl.when(cross & (p == 1))
        def _():
            chip_copy(r).wait_recv()
            chip_copy(u).wait_recv()
            attend(r, u, NZ)

        @pl.when(jnp.logical_not(cross))
        def _():
            @pl.when((at > 0) & (p == 1))
            def _():
                pl.when(at > 1)(lambda: pass_on(2 * at))
                pass_on(2 * at + 1)

            attend(r, u, 0)

        return carry

    lax.fori_loop(0, NZ, step, 0)

    whole = jnp.sum(totals[...], axis=0, keepdims=True)
    some = whole > 0.0
    inverse = 1.0 / jnp.where(some, whole, 1.0)
    level = jnp.where(some, tops[...] + jnp.log2(jnp.where(some, whole, 1.0)), NOTHING)
    for j in range(SLOTS):
        for xx in range(NX):
            at = j * NX + xx
            cols = slice(at * TILE, (at + 1) * TILE)
            stat_v[xx, j:j + 1, :] = level[:, cols]

    def stat_copy(d):
        return remote(
            stat_v.at[(x + d) % NX], part_stats.at[d - 1], s_send.at[d - 1], s_recv.at[d - 1], along_x(d)
        )

    def part_copy(j, d):
        at = 3 * j + d - 1
        return remote(
            o_v.at[j * NX + (x + d) % NX], parts.at[at], x_send.at[at], x_recv.at[at], along_x(d)
        )

    for d in range(1, NX):
        stat_copy(d).start()
    for j in range(SLOTS):
        row, live = live_slot(j)

        @pl.when(live)
        def _():
            for xx in range(NX):
                at = j * NX + xx
                cols = slice(at * TILE, (at + 1) * TILE)
                o_v[at] = (acc[:, cols] * inverse[:, cols]).astype(BF16)
            for d in range(1, NX):
                part_copy(j, d).start()

    for d in range(1, NY):
        for part in range(2):
            w_arrival(d, part).wait_recv()
        w_swap(d, rows_mine).start()

    def back(j):
        row, live = live_slot(j)
        dst = full.at[3 * y + g]
        away = remote(merged.at[j], dst, o_send.at[j], o_recv.at[g], dev(seq=x * NZ + row))
        here = pltpu.make_async_copy(merged.at[j], dst, o_send.at[j])
        return row, live, away, here

    for d in range(1, NX):
        stat_copy(d).wait_recv()
    for j in range(SLOTS):
        row, live, away, here = back(j)

        @pl.when(live)
        def _():
            stats = [stat_v[x, j:j + 1, :]] + [part_stats[d, j:j + 1, :] for d in range(3)]
            top = functools.reduce(jnp.maximum, stats)
            shares = [jnp.exp2(stat - top) for stat in stats]
            share_sum = sum(shares)
            for d in range(1, NX):
                part_copy(j, d).wait_recv()
            blocks = [o_v[j * NX + x]] + [parts[3 * j + d] for d in range(3)]
            mixed = sum(block.astype(F32) * (share / share_sum) for block, share in zip(blocks, shares))
            merged[j] = mixed.T.astype(BF16)
            pl.when(row != z)(away.start)
            pl.when(row == z)(here.start)

    def y_copy(n, d):
        block = full.at[3 * y + n]
        return remote(block, block, y_send.at[3 * n + d - 1], y_recv.at[3 * n + d - 1], along_y(d))

    def y_arrival(n, d):
        block = full.at[3 * ((y + NY - d) % NY) + n]
        return remote(block, block, y_send.at[3 * n + d - 1], y_recv.at[3 * n + d - 1], along_y(d))

    for j in range(SLOTS):
        row, live, away, here = back(j)
        pl.when(live & (row == z))(here.wait)

    for n in range(3):
        row, _slot = query_place(z, n)
        block = full.at[3 * y + n]
        pl.when(row != z)(remote(block, block, o_send.at[0], o_recv.at[n], dev()).wait_recv)
        for d in range(1, NY):
            y_copy(n, d).start()

    for load in loads[6:]:
        load.wait()
    for d in range(1, NY):
        w_swap(d, rows_other).wait_recv()
    for n in range(3):
        for d in range(1, NY):
            y_arrival(n, d).wait_recv()

    def projected(part):
        total = jnp.zeros((TILE, 3 * HD), F32)
        for n in range(3 * NY):
            weights = w_v[n // 3, n % 3 * HD:(n % 3 + 1) * HD, part_cols(part)]
            total = total + jnp.dot(full[n], weights, preferred_element_type=F32)
        return total

    give[...] = projected(1).astype(BF16)
    swap = remote(give, got, h_send, h_recv, partner)
    swap.start()
    own = projected(0)
    swap.wait_recv()
    out_ref[...] = (own + got[...].astype(F32)).astype(BF16)

    def drain(r, carry):
        place = kv.at[r]
        pl.when((r < z) & (z < b))(up_copy(r, place, zf_send.at[r]).wait_send)
        pl.when((r > z) & (z > a))(down_copy(r, place, zf_send.at[r]).wait_send)
        pl.when(p == 0)(chip_copy(r).wait_send)
        return carry

    lax.fori_loop(0, NZ, drain, 0)
    pl.when(z < b)(up_copy(z, mine.at[g], z_send.at[3]).wait_send)
    pl.when(z > a)(down_copy(z, mine.at[g], z_send.at[4]).wait_send)
    for n in range(3):
        e, copy = entry_copy(n)
        pl.when((e != z) & (p == 1))(copy.wait_send)
        row, away, here = query_copies(n)
        pl.when(row != z)(away.wait_send)

    for j in range(SLOTS):
        row, live, away, here = back(j)

        @pl.when(live)
        def _():
            for d in range(1, NX):
                qx_copy(j, d).wait_send()
                part_copy(j, d).wait_send()
            pl.when(row != z)(away.wait_send)

    for d in range(1, NX):
        stat_copy(d).wait_send()
    for d in range(1, NY):
        for part in range(2):
            w_copy(d, part).wait_send()
        w_swap(d, rows_mine).wait_send()
        for n in range(3):
            y_copy(n, d).wait_send()
    swap.wait_send()


def on_device(queries, keys, values, self_pairs, mask_pairs, counts, out_weight):
    hbm = pl.BlockSpec(memory_space=pltpu.HBM)
    vmem = pltpu.VMEM
    dma = pltpu.SemaphoreType.DMA
    rows = (TILE, 3 * HD)
    projected = pl.pallas_call(
        layer_kernel,
        out_shape=jax.ShapeDtypeStruct(rows, BF16),
        in_specs=[hbm] * 7,
        out_specs=pl.BlockSpec(memory_space=vmem),
        scratch_shapes=[
            vmem(rows, BF16), vmem(rows, BF16), vmem(rows, BF16),
            vmem((2, 2, self_pairs.shape[1]), I32), vmem((2, mask_pairs.shape[0]), I32), pltpu.SMEM((3,), I32),
            vmem((3, 2 * TILE, HD), BF16),
            vmem((ENTRIES, 2 * TILE, HD), BF16),
            vmem((NX * SLOTS, TILE, HD), BF16),
            vmem((HD, QUERIES), BF16),
            vmem((ENTRIES, QUERIES), F32),
            vmem((1, QUERIES), F32),
            vmem((8, QUERIES), F32),
            vmem((HD, QUERIES), F32),
            vmem((NY, 3 * HD, 6 * HD), BF16),
            vmem((NX * SLOTS, HD, TILE), BF16),
            vmem((NX, 8, TILE), F32),
            vmem((3 * SLOTS, HD, TILE), BF16),
            vmem((3, 8, TILE), F32),
            vmem((SLOTS, TILE, HD), BF16),
            vmem((3 * NY, TILE, HD), BF16),
            vmem(rows, BF16), vmem(rows, BF16),
            dma((5,)), dma((NZ,)), dma((NZ,)), dma((NZ,)), dma((NZ,)),
            dma((3,)), dma((SLOTS,)), dma((3 * SLOTS,)), dma((3 * SLOTS,)),
            dma((2 * NY,)), dma((2 * NY,)), dma((NY,)), dma((NY,)),
            dma((3 * SLOTS,)), dma((3 * SLOTS,)), dma((3,)), dma((3,)),
            dma((SLOTS,)), dma((3,)), dma((9,)), dma((9,)), dma, dma, pltpu.SemaphoreType.REGULAR, dma((8,)),
        ],
        compiler_params=pltpu.CompilerParams(
            collective_id=0, has_side_effects=True, vmem_limit_bytes=60 * 1024 * 1024
        ),
        name="layer",
    )(
        counts, queries[0], keys[0], values[0],
        jnp.swapaxes(self_pairs, 1, 2), jnp.swapaxes(mask_pairs, 0, 1), out_weight,
    )
    return projected[None]


def solution(mesh):
    in_specs = (
        P("pass", "seq", "head"),
        P("pass", "seq", "head"),
        P("pass", "seq", "head"),
        P(),
        P(),
        P(),
        P("head", None),
    )
    out_specs = P("pass", "seq", "head")
    return jax.shard_map(
        on_device, mesh=mesh, in_specs=in_specs, out_specs=out_specs, check_vma=False
    )
```

```python
import functools
import math

import jax
import jax.numpy as jnp
from jax import lax
from jax.experimental import pallas as pl
from jax.experimental.pallas import tpu as pltpu
from jax.sharding import PartitionSpec as P

HD = 128
TILE = 128
NX = 4
NZ = 8
NY = 4
SLOTS = 4
ENTRIES = 2 * NZ
BF16 = jnp.bfloat16
F32 = jnp.float32
I32 = jnp.int32
EXP2_SCALE = HD ** -0.5 * math.log2(math.e)
NOTHING = -1e30
QUERIES = NX * SLOTS * TILE
MESH = pl.DeviceIdType.MESH


def head_of_row(z):
    return (3 * z + 1) // 8


def first_row(g):
    return (8 * g + 1) // 3


def last_row(g):
    return (8 * g + 9) // 3 - 1


def query_place(zq, g):
    if g == 0:
        return zq // 3, zq % 3
    if g == 1:
        return 3 + zq // 4, zq % 4
    return 7 - (7 - zq) // 3, (7 - zq) % 3


def slot_row(z, g, j):
    low = 3 * z + j
    mid = 4 * (z - 3) + j
    high = 7 - (3 * (7 - z) + j)
    row = jnp.where(g == 0, low, jnp.where(g == 1, mid, high))
    return jnp.where((j == 3) & (g != 1), -1, row)


def row_order(i, z):
    near = jnp.minimum(z, 7 - z)
    d = (i + 1) // 2
    both = z + d * (1 - 2 * (i % 2))
    return jnp.where(i <= 2 * near, both, jnp.where(z <= 3, i, 7 - i))


def remote(src, dst, send, recv, target):
    return pltpu.make_async_remote_copy(
        src_ref=src, dst_ref=dst, send_sem=send, recv_sem=recv, device_id=target, device_id_type=MESH
    )


def layer_kernel(
    counts_ref, q_ref, k_ref, v_ref, sp_ref, mp_ref, w_ref, out_ref,
    q_v, k_v, v_v, sp_v, mp_v, counts_v,
    mine, kv, qs, qt, bias, tops, totals, acc, w_v,
    o_v, stat_v, parts, part_stats, merged, full, give, got,
    z_send, z_recv, zf_send, c_send, c_recv,
    q_send, q_recv, qx_send, qx_recv, w_send, w_recv, wc_send, wc_recv,
    x_send, x_recv, s_send, s_recv, o_send, o_recv, y_send, y_recv, h_send, h_recv, turn, local_sem,
):
    s = lax.axis_index("seq")
    p = lax.axis_index("pass")
    h = lax.axis_index("head")
    x, z = s // NZ, s % NZ
    zh, y = h // NY, h % NY
    g = head_of_row(z)
    a, b = first_row(g), last_row(g)

    def dev(seq=s, core=p, head=h):
        return {"seq": seq, "pass": core, "head": head}

    def along_x(d):
        return dev(seq=((x + d) % NX) * NZ + z)

    def along_y(d):
        return dev(head=zh * NY + (y + d) % NY)

    partner = dev(head=(1 - zh) * NY + y)
    met = (
        [dev(seq=x * NZ + (z + d) % NZ) for d in range(1, NZ)]
        + [along_x(d) for d in range(1, NX)]
        + [along_y(d) for d in range(1, NY)]
        + [dev(core=1 - p), partner]
    )
    barrier = pltpu.get_barrier_semaphore()
    for device in met:
        pl.semaphore_signal(barrier, inc=1, device_id=device, device_id_type=MESH)

    def w_cols(yy, part):
        zz = zh if part == 0 else 1 - zh
        return pl.ds(pl.multiple_of((zz * NY + yy) * (3 * HD), 3 * HD), 3 * HD)

    def part_cols(part):
        return slice(part * 3 * HD, (part + 1) * 3 * HD)

    loads = [
        pltpu.make_async_copy(src, dst, local_sem.at[i])
        for i, (src, dst) in enumerate(
            [(k_ref, k_v), (v_ref, v_v), (q_ref, q_v), (counts_ref, counts_v), (sp_ref, sp_v), (mp_ref, mp_v)]
            + [(w_ref.at[:, w_cols(y, part)], w_v.at[y, :, part_cols(part)]) for part in range(2)]
        )
    ]
    for load in loads:
        load.start()

    loads[0].wait()
    loads[1].wait()
    for n in range(3):
        cols = slice(n * HD, (n + 1) * HD)
        mine[n, :TILE, :] = k_v[:, cols]
        mine[n, TILE:, :] = v_v[:, cols].T
    kv[z] = mine[g]
    loads[2].wait()

    pl.semaphore_wait(barrier, len(met))

    def query_copies(n):
        row, slot = query_place(z, n)
        src, dst = q_v.at[:, n * HD:(n + 1) * HD], qs.at[slot * NX + x]
        away = remote(src, dst, q_send.at[n], q_recv.at[slot], dev(seq=x * NZ + row))
        here = pltpu.make_async_copy(src, dst, q_send.at[n])
        return row, away, here

    for n in range(3):
        row, away, here = query_copies(n)
        pl.when(row != z)(away.start)
        pl.when(row == z)(here.start)

    def up_copy(r, src, send):
        return remote(src, kv.at[r], send, z_recv.at[r], dev(seq=s + 1))

    def down_copy(r, src, send):
        return remote(src, kv.at[r], send, z_recv.at[r], dev(seq=s - 1))

    def entry_copy(n):
        e = jnp.maximum(first_row(n), jnp.minimum(z, last_row(n)))
        return e, remote(mine.at[n], kv.at[z], z_send.at[n], z_recv.at[z], dev(seq=x * NZ + e))

    pl.when(z < b)(up_copy(z, mine.at[g], z_send.at[3]).start)
    pl.when(z > a)(down_copy(z, mine.at[g], z_send.at[4]).start)
    def later(e):
        return (p == 1) & ((e - z) * (e - z) > 1)

    for n in range(3):
        e, copy = entry_copy(n)
        pl.when((e != z) & jnp.logical_not(later(e)))(copy.start)

    half_rows = 3 * HD // 2
    rows_mine = pl.ds(pl.multiple_of(p * half_rows, half_rows), half_rows)
    rows_other = pl.ds(pl.multiple_of((1 - p) * half_rows, half_rows), half_rows)

    def w_copy(d, part):
        return remote(
            w_ref.at[rows_mine, w_cols((y + d) % NY, part)], w_v.at[y, rows_mine, part_cols(part)],
            w_send.at[2 * d + part], w_recv.at[2 * d + part], along_y(d),
        )

    def w_arrival(d, part):
        place = w_v.at[(y + NY - d) % NY, rows_mine, part_cols(part)]
        return remote(place, place, w_send.at[2 * d + part], w_recv.at[2 * d + part], along_y(d))

    def w_swap(d, rows):
        place = w_v.at[(y + NY - d) % NY, rows]
        return remote(place, place, wc_send.at[d], wc_recv.at[d], dev(core=1 - p))

    for part in range(2):
        for d in range(1, NY):
            w_copy(d, part).start()

    for load in loads[3:6]:
        load.wait()
    slots = lax.broadcasted_iota(I32, (NX * SLOTS, 1), 0)
    tiles = jnp.full((NX * SLOTS, 1), -1, I32)
    for j in range(SLOTS):
        row = slot_row(z, g, j)
        live = (row >= 0) & (row < NZ)
        tiles = jnp.where(((slots >> 2) == j) & live, (slots & 3) * NZ + row, tiles)

    def hits(queries, keys, live_count, shift):
        live = lax.broadcasted_iota(I32, queries.shape, 1) < live_count
        row_hits = ((queries == tiles) & live).astype(F32)
        row = keys - x * NZ
        row = jnp.where((row >= 0) & (row < NZ), row + shift, -1)
        col_hits = (lax.broadcasted_iota(I32, (ENTRIES, 1), 0) == row).astype(F32)
        return lax.dot_general(col_hits, row_hits, (((1,), (1,)), ((), ())), preferred_element_type=F32)

    is_edit = (p == 1).astype(F32)
    counted = hits(sp_v[p, 0:1], sp_v[p, 1:2], counts_v[p], 0)
    counted = counted + is_edit * hits(mp_v[0:1], mp_v[1:2], counts_v[2], NZ)
    allowed = (counted > 0.5).astype(F32)
    spread = lax.broadcasted_iota(I32, (NX * SLOTS, QUERIES), 1) // TILE
    spread = (spread == lax.broadcasted_iota(I32, (NX * SLOTS, QUERIES), 0)).astype(F32)
    live = jnp.dot(allowed, spread, preferred_element_type=F32)
    bias[...] = jnp.where(live > 0.5, 0.0, NOTHING)
    tops[...] = jnp.full(tops.shape, NOTHING, F32)
    totals[...] = jnp.zeros(totals.shape, F32)
    acc[...] = jnp.zeros(acc.shape, F32)

    def chip_copy(r):
        return remote(kv.at[r], kv.at[NZ + r], c_send.at[r], c_recv.at[r], dev(core=1 - p))

    pl.when(p == 0)(chip_copy(z).start)

    def pass_on(i):
        r = row_order(i, z)
        place = kv.at[r]
        remote(place, place, z_send.at[0], z_recv.at[r], dev()).wait_recv()
        pl.when((r < z) & (z < b))(up_copy(r, place, zf_send.at[r]).start)
        pl.when((r > z) & (z > a))(down_copy(r, place, zf_send.at[r]).start)
        pl.when(p == 0)(chip_copy(r).start)

    def qx_copy(j, d):
        place = qs.at[j * NX + x]
        return remote(place, place, qx_send.at[3 * j + d - 1], qx_recv.at[3 * j + d - 1], along_x(d))

    def qx_arrival(j, d):
        place = qs.at[j * NX + (x + NX - d) % NX]
        return remote(place, place, qx_send.at[3 * j + d - 1], qx_recv.at[3 * j + d - 1], along_x(d))

    def live_slot(j):
        row = slot_row(z, g, j)
        return row, (row >= 0) & (row < NZ)

    for n in range(3):
        row, away, here = query_copies(n)
        pl.when(row == z)(here.wait)

    for j in range(SLOTS):
        row, live = live_slot(j)
        place = qs.at[j * NX + x]

        @pl.when(live)
        def _():
            pl.when(row != z)(remote(place, place, q_send.at[0], q_recv.at[j], dev()).wait_recv)
            for d in (2, 1, 3):
                qx_copy(j, d).start()

    pass_on(1)

    pass_on(2)

    @pl.when(p == 0)
    def _():
        for n in range(2):
            pl.when((g == 1) == (n == 0))(entry_copy(n)[1].wait_send)
        pl.semaphore_signal(turn, inc=1, device_id=dev(core=1), device_id_type=MESH)

        def passing(i, carry):
            pass_on(i)
            return carry

        lax.fori_loop(3, NZ, passing, 0)

    @pl.when(p == 1)
    def _():
        pl.semaphore_wait(turn, 1)
        for n in range(3):
            e, copy = entry_copy(n)
            pl.when(later(e))(copy.start)

    for j in range(SLOTS):
        row, live = live_slot(j)

        @pl.when(live)
        def _():
            for d in range(1, NX):
                qx_arrival(j, d).wait_recv()
            for xx in range(NX):
                at = j * NX + xx
                qt[:, at * TILE:(at + 1) * TILE] = qs[at].T

    live_slots = jnp.where(g == 1, 4, jnp.where((z == 2) | (z == 5), 2, 3))

    def attend(r, u, base):
        for width in range(2, SLOTS + 1):
            pl.when(live_slots == width)(functools.partial(attend_slots, r, u, base, width * NX * TILE))

    def attend_slots(r, u, base, width):
        cols = slice(0, width)
        keys = jnp.concatenate([kv[base + r, :TILE, :], kv[base + u, :TILE, :]], axis=0)
        values = jnp.concatenate([kv[base + r, TILE:, :], kv[base + u, TILE:, :]], axis=1)
        scores = jnp.dot(keys, qt[:, cols], preferred_element_type=F32)
        first, second = scores[:TILE], scores[TILE:]
        first_bias = bias[pl.ds(base + r, 1), cols]
        second_bias = bias[pl.ds(base + u, 1), cols]
        top = tops[:, cols]
        new_top = jnp.maximum(top, jnp.maximum(
            jnp.max(first, axis=0, keepdims=True) * EXP2_SCALE + first_bias,
            jnp.max(second, axis=0, keepdims=True) * EXP2_SCALE + second_bias,
        ))
        level = jnp.maximum(new_top, NOTHING / 10)
        faded = jnp.exp2(top - new_top)
        first = jnp.exp2(first * EXP2_SCALE - (level - first_bias))
        second = jnp.exp2(second * EXP2_SCALE - (level - second_bias))
        tops[:, cols] = new_top
        totals[:, cols] = totals[:, cols] * faded + jnp.sum((first + second).reshape(16, 8, width), axis=0)
        weights = jnp.concatenate([first.astype(BF16), second.astype(BF16)], axis=0)
        acc[:, cols] = acc[:, cols] * faded + jnp.dot(values, weights, preferred_element_type=F32)

    def step(i, carry):
        cross = (i != 1) & (i < 5)
        at = jnp.where(i < 2, 0, jnp.where(i < 5, i - 1, i - 4))
        r, u = row_order(2 * at, z), row_order(2 * at + 1, z)

        @pl.when(cross & (p == 1))
        def _():
            chip_copy(r).wait_recv()
            chip_copy(u).wait_recv()
            attend(r, u, NZ)

        @pl.when(jnp.logical_not(cross))
        def _():
            @pl.when((at > 0) & (p == 1))
            def _():
                pl.when(at > 1)(lambda: pass_on(2 * at))
                pass_on(2 * at + 1)

            attend(r, u, 0)

        return carry

    lax.fori_loop(0, NZ, step, 0)

    whole = jnp.sum(totals[...], axis=0, keepdims=True)
    some = whole > 0.0
    inverse = 1.0 / jnp.where(some, whole, 1.0)
    level = jnp.where(some, tops[...] + jnp.log2(jnp.where(some, whole, 1.0)), NOTHING)
    for j in range(SLOTS):
        for xx in range(NX):
            at = j * NX + xx
            cols = slice(at * TILE, (at + 1) * TILE)
            stat_v[xx, j:j + 1, :] = level[:, cols]

    def stat_copy(d):
        return remote(
            stat_v.at[(x + d) % NX], part_stats.at[d - 1], s_send.at[d - 1], s_recv.at[d - 1], along_x(d)
        )

    def part_copy(j, d):
        at = 3 * j + d - 1
        return remote(
            o_v.at[j * NX + (x + d) % NX], parts.at[at], x_send.at[at], x_recv.at[at], along_x(d)
        )

    for d in range(1, NX):
        stat_copy(d).start()
    for j in range(SLOTS):
        row, live = live_slot(j)

        @pl.when(live)
        def _():
            for xx in range(NX):
                at = j * NX + xx
                cols = slice(at * TILE, (at + 1) * TILE)
                o_v[at] = (acc[:, cols] * inverse[:, cols]).astype(BF16)
            for d in (2, 1, 3):
                part_copy(j, d).start()

    for d in range(1, NY):
        for part in range(2):
            w_arrival(d, part).wait_recv()
        w_swap(d, rows_mine).start()

    def back(j):
        row, live = live_slot(j)
        dst = full.at[3 * y + g]
        away = remote(merged.at[j], dst, o_send.at[j], o_recv.at[g], dev(seq=x * NZ + row))
        here = pltpu.make_async_copy(merged.at[j], dst, o_send.at[j])
        return row, live, away, here

    for d in range(1, NX):
        stat_copy(d).wait_recv()
    for j in range(SLOTS):
        row, live, away, here = back(j)

        @pl.when(live)
        def _():
            stats = [stat_v[x, j:j + 1, :]] + [part_stats[d, j:j + 1, :] for d in range(3)]
            top = functools.reduce(jnp.maximum, stats)
            shares = [jnp.exp2(stat - top) for stat in stats]
            share_sum = sum(shares)
            for d in range(1, NX):
                part_copy(j, d).wait_recv()
            blocks = [o_v[j * NX + x]] + [parts[3 * j + d] for d in range(3)]
            mixed = sum(block.astype(F32) * (share / share_sum) for block, share in zip(blocks, shares))
            merged[j] = mixed.T.astype(BF16)
            pl.when(row != z)(away.start)
            pl.when(row == z)(here.start)

    def y_copy(n, d):
        block = full.at[3 * y + n]
        return remote(block, block, y_send.at[3 * n + d - 1], y_recv.at[3 * n + d - 1], along_y(d))

    def y_arrival(n, d):
        block = full.at[3 * ((y + NY - d) % NY) + n]
        return remote(block, block, y_send.at[3 * n + d - 1], y_recv.at[3 * n + d - 1], along_y(d))

    for j in range(SLOTS):
        row, live, away, here = back(j)
        pl.when(live & (row == z))(here.wait)

    for n in range(3):
        row, _slot = query_place(z, n)
        block = full.at[3 * y + n]
        pl.when(row != z)(remote(block, block, o_send.at[0], o_recv.at[n], dev()).wait_recv)
        for d in (2, 1, 3):
            y_copy(n, d).start()

    for load in loads[6:]:
        load.wait()
    for d in range(1, NY):
        w_swap(d, rows_other).wait_recv()
    def projected(n, d, part):
        at = (y + NY - d) % NY
        return jnp.dot(
            full[3 * at + n], w_v[at, n * HD:(n + 1) * HD, part_cols(part)], preferred_element_type=F32
        )

    theirs = sum(projected(n, 0, 1) for n in range(3))
    for n in range(3):
        for d in range(1, NY):
            y_arrival(n, d).wait_recv()
            theirs = theirs + projected(n, d, 1)
    give[...] = theirs.astype(BF16)
    swap = remote(give, got, h_send, h_recv, partner)
    swap.start()
    own = sum(projected(n, d, 0) for n in range(3) for d in range(NY))
    swap.wait_recv()
    out_ref[...] = (own + got[...].astype(F32)).astype(BF16)

    def drain(r, carry):
        place = kv.at[r]
        pl.when((r < z) & (z < b))(up_copy(r, place, zf_send.at[r]).wait_send)
        pl.when((r > z) & (z > a))(down_copy(r, place, zf_send.at[r]).wait_send)
        pl.when(p == 0)(chip_copy(r).wait_send)
        return carry

    lax.fori_loop(0, NZ, drain, 0)
    pl.when(z < b)(up_copy(z, mine.at[g], z_send.at[3]).wait_send)
    pl.when(z > a)(down_copy(z, mine.at[g], z_send.at[4]).wait_send)
    for n in range(3):
        e, copy = entry_copy(n)
        waited = (p == 0) & ((g == 1) if n == 0 else (g != 1) & (n == 1))
        pl.when((e != z) & jnp.logical_not(waited))(copy.wait_send)
        row, away, here = query_copies(n)
        pl.when(row != z)(away.wait_send)

    for j in range(SLOTS):
        row, live, away, here = back(j)

        @pl.when(live)
        def _():
            for d in range(1, NX):
                qx_copy(j, d).wait_send()
                part_copy(j, d).wait_send()
            pl.when(row != z)(away.wait_send)

    for d in range(1, NX):
        stat_copy(d).wait_send()
    for d in range(1, NY):
        for part in range(2):
            w_copy(d, part).wait_send()
        w_swap(d, rows_mine).wait_send()
        for n in range(3):
            y_copy(n, d).wait_send()
    swap.wait_send()


def on_device(queries, keys, values, self_pairs, mask_pairs, counts, out_weight):
    hbm = pl.BlockSpec(memory_space=pltpu.HBM)
    vmem = pltpu.VMEM
    dma = pltpu.SemaphoreType.DMA
    rows = (TILE, 3 * HD)
    projected = pl.pallas_call(
        layer_kernel,
        out_shape=jax.ShapeDtypeStruct(rows, BF16),
        in_specs=[hbm] * 7,
        out_specs=pl.BlockSpec(memory_space=vmem),
        scratch_shapes=[
            vmem(rows, BF16), vmem(rows, BF16), vmem(rows, BF16),
            vmem((2, 2, self_pairs.shape[1]), I32), vmem((2, mask_pairs.shape[0]), I32), pltpu.SMEM((3,), I32),
            vmem((3, 2 * TILE, HD), BF16),
            vmem((ENTRIES, 2 * TILE, HD), BF16),
            vmem((NX * SLOTS, TILE, HD), BF16),
            vmem((HD, QUERIES), BF16),
            vmem((ENTRIES, QUERIES), F32),
            vmem((1, QUERIES), F32),
            vmem((8, QUERIES), F32),
            vmem((HD, QUERIES), F32),
            vmem((NY, 3 * HD, 6 * HD), BF16),
            vmem((NX * SLOTS, HD, TILE), BF16),
            vmem((NX, 8, TILE), F32),
            vmem((3 * SLOTS, HD, TILE), BF16),
            vmem((3, 8, TILE), F32),
            vmem((SLOTS, TILE, HD), BF16),
            vmem((3 * NY, TILE, HD), BF16),
            vmem(rows, BF16), vmem(rows, BF16),
            dma((5,)), dma((NZ,)), dma((NZ,)), dma((NZ,)), dma((NZ,)),
            dma((3,)), dma((SLOTS,)), dma((3 * SLOTS,)), dma((3 * SLOTS,)),
            dma((2 * NY,)), dma((2 * NY,)), dma((NY,)), dma((NY,)),
            dma((3 * SLOTS,)), dma((3 * SLOTS,)), dma((3,)), dma((3,)),
            dma((SLOTS,)), dma((3,)), dma((9,)), dma((9,)), dma, dma, pltpu.SemaphoreType.REGULAR, dma((8,)),
        ],
        compiler_params=pltpu.CompilerParams(
            collective_id=0, has_side_effects=True, vmem_limit_bytes=32 * 1024 * 1024
        ),
        name="layer",
    )(*[
        pltpu.with_memory_space_constraint(each, pltpu.HBM)
        for each in (
            counts, queries[0], keys[0], values[0],
            jnp.swapaxes(self_pairs, 1, 2), jnp.swapaxes(mask_pairs, 0, 1), out_weight,
        )
    ])
    return projected[None]


def solution(mesh):
    in_specs = (
        P("pass", "seq", "head"),
        P("pass", "seq", "head"),
        P("pass", "seq", "head"),
        P(),
        P(),
        P(),
        P("head", None),
    )
    out_specs = P("pass", "seq", "head")
    return jax.shard_map(
        on_device, mesh=mesh, in_specs=in_specs, out_specs=out_specs, check_vma=False
    )
```

```python
import functools
import math

import jax
import jax.numpy as jnp
from jax import lax
from jax.experimental import pallas as pl
from jax.experimental.pallas import tpu as pltpu
from jax.sharding import PartitionSpec as P

HD = 128
TILE = 128
NX = 4
NZ = 8
NY = 4
SLOTS = 4
ENTRIES = 2 * NZ
BF16 = jnp.bfloat16
F32 = jnp.float32
I32 = jnp.int32
EXP2_SCALE = HD ** -0.5 * math.log2(math.e)
NOTHING = -1e30
QUERIES = NX * SLOTS * TILE
MESH = pl.DeviceIdType.MESH


def head_of_row(z):
    return (3 * z + 1) // 8


def first_row(g):
    return (8 * g + 1) // 3


def last_row(g):
    return (8 * g + 9) // 3 - 1


def query_place(zq, g):
    if g == 0:
        return zq // 3, zq % 3
    if g == 1:
        return 3 + zq // 4, zq % 4
    return 7 - (7 - zq) // 3, (7 - zq) % 3


def slot_row(z, g, j):
    low = 3 * z + j
    mid = 4 * (z - 3) + j
    high = 7 - (3 * (7 - z) + j)
    row = jnp.where(g == 0, low, jnp.where(g == 1, mid, high))
    return jnp.where((j == 3) & (g != 1), -1, row)


def row_order(i, z):
    near = jnp.minimum(z, 7 - z)
    d = (i + 1) // 2
    both = z + d * (1 - 2 * (i % 2))
    return jnp.where(i <= 2 * near, both, jnp.where(z <= 3, i, 7 - i))


def remote(src, dst, send, recv, target):
    return pltpu.make_async_remote_copy(
        src_ref=src, dst_ref=dst, send_sem=send, recv_sem=recv, device_id=target, device_id_type=MESH
    )


class Copies:
    def __init__(self, copies):
        self.copies = copies

    def start(self):
        for copy in self.copies:
            copy.start()

    def wait_send(self):
        for copy in self.copies:
            copy.wait_send()


def layer_kernel(
    counts_ref, q_ref, k_ref, v_ref, sp_ref, mp_ref, w_ref, out_ref,
    q_v, k_v, v_v, sp_v, mp_v, counts_v,
    mine, kv, qs, qt, bias, tops, totals, acc, w_v,
    o_v, stat_v, parts, part_stats, merged, full, give, got,
    z_send, z_recv, zf_send, c_send, c_recv,
    q_send, q_recv, qx_send, qx_recv, w_send, w_recv, wc_send, wc_recv,
    x_send, x_recv, s_send, s_recv, o_send, o_recv, y_send, y_recv, h_send, h_recv, turn, local_sem,
):
    s = lax.axis_index("seq")
    p = lax.axis_index("pass")
    h = lax.axis_index("head")
    x, z = s // NZ, s % NZ
    zh, y = h // NY, h % NY
    g = head_of_row(z)
    a, b = first_row(g), last_row(g)

    def dev(seq=s, core=p, head=h):
        return {"seq": seq, "pass": core, "head": head}

    def along_x(d):
        return dev(seq=((x + d) % NX) * NZ + z)

    def along_y(d):
        return dev(head=zh * NY + (y + d) % NY)

    partner = dev(head=(1 - zh) * NY + y)
    met = (
        [dev(seq=x * NZ + (z + d) % NZ) for d in range(1, NZ)]
        + [along_x(d) for d in range(1, NX)]
        + [along_y(d) for d in range(1, NY)]
        + [dev(core=1 - p), partner]
    )
    barrier = pltpu.get_barrier_semaphore()
    for device in met:
        pl.semaphore_signal(barrier, inc=1, device_id=device, device_id_type=MESH)

    def w_cols(yy, part):
        zz = zh if part == 0 else 1 - zh
        return pl.ds(pl.multiple_of((zz * NY + yy) * (3 * HD), 3 * HD), 3 * HD)

    def part_cols(part):
        return slice(part * 3 * HD, (part + 1) * 3 * HD)

    loads = [
        pltpu.make_async_copy(src, dst, local_sem.at[i])
        for i, (src, dst) in enumerate(
            [(k_ref, k_v), (v_ref, v_v), (q_ref, q_v), (counts_ref, counts_v), (sp_ref, sp_v), (mp_ref, mp_v)]
            + [(w_ref.at[:, w_cols(y, part)], w_v.at[y, :, part_cols(part)]) for part in range(2)]
        )
    ]
    for load in loads:
        load.start()

    loads[0].wait()
    loads[1].wait()
    for n in range(3):
        cols = slice(n * HD, (n + 1) * HD)
        mine[n, :TILE, :] = k_v[:, cols]
        mine[n, TILE:, :] = v_v[:, cols].T
    kv[z] = mine[g]
    loads[2].wait()

    pl.semaphore_wait(barrier, len(met))

    def query_copies(n):
        row, slot = query_place(z, n)
        src, dst = q_v.at[:, n * HD:(n + 1) * HD], qs.at[slot * NX + x]
        away = remote(src, dst, q_send.at[n], q_recv.at[slot], dev(seq=x * NZ + row))
        here = pltpu.make_async_copy(src, dst, q_send.at[n])
        return row, away, here

    for n in range(3):
        row, away, here = query_copies(n)
        pl.when(row != z)(away.start)
        pl.when(row == z)(here.start)

    def two_copies(r, src, sems, at, target):
        return Copies([
            remote(src.at[part], kv.at[r].at[part], sems.at[2 * at + k], z_recv.at[2 * r + k], target)
            for k, part in enumerate((slice(0, TILE), slice(TILE, 2 * TILE)))
        ])

    def up_copy(r, src, sems, at):
        return two_copies(r, src, sems, at, dev(seq=s + 1))

    def down_copy(r, src, sems, at):
        return two_copies(r, src, sems, at, dev(seq=s - 1))

    def entry_copy(n):
        e = jnp.maximum(first_row(n), jnp.minimum(z, last_row(n)))
        return e, two_copies(z, mine.at[n], z_send, n, dev(seq=x * NZ + e))

    pl.when(z < b)(up_copy(z, mine.at[g], z_send, 3).start)
    pl.when(z > a)(down_copy(z, mine.at[g], z_send, 4).start)
    def later(e):
        return (p == 1) & ((e - z) * (e - z) > 1)

    for n in range(3):
        e, copy = entry_copy(n)
        pl.when((e != z) & jnp.logical_not(later(e)))(copy.start)

    half_rows = 3 * HD // 2
    rows_mine = pl.ds(pl.multiple_of(p * half_rows, half_rows), half_rows)
    rows_other = pl.ds(pl.multiple_of((1 - p) * half_rows, half_rows), half_rows)

    def w_copy(d, part):
        return remote(
            w_ref.at[rows_mine, w_cols((y + d) % NY, part)], w_v.at[y, rows_mine, part_cols(part)],
            w_send.at[2 * d + part], w_recv.at[2 * d + part], along_y(d),
        )

    def w_arrival(d, part):
        place = w_v.at[(y + NY - d) % NY, rows_mine, part_cols(part)]
        return remote(place, place, w_send.at[2 * d + part], w_recv.at[2 * d + part], along_y(d))

    def w_swap(d, rows):
        place = w_v.at[(y + NY - d) % NY, rows]
        return remote(place, place, wc_send.at[d], wc_recv.at[d], dev(core=1 - p))

    for part in range(2):
        for d in range(1, NY):
            w_copy(d, part).start()

    for load in loads[3:6]:
        load.wait()
    slots = lax.broadcasted_iota(I32, (NX * SLOTS, 1), 0)
    tiles = jnp.full((NX * SLOTS, 1), -1, I32)
    for j in range(SLOTS):
        row = slot_row(z, g, j)
        live = (row >= 0) & (row < NZ)
        tiles = jnp.where(((slots >> 2) == j) & live, (slots & 3) * NZ + row, tiles)

    def hits(queries, keys, live_count, shift):
        live = lax.broadcasted_iota(I32, queries.shape, 1) < live_count
        row_hits = ((queries == tiles) & live).astype(F32)
        row = keys - x * NZ
        row = jnp.where((row >= 0) & (row < NZ), row + shift, -1)
        col_hits = (lax.broadcasted_iota(I32, (ENTRIES, 1), 0) == row).astype(F32)
        return lax.dot_general(col_hits, row_hits, (((1,), (1,)), ((), ())), preferred_element_type=F32)

    is_edit = (p == 1).astype(F32)
    counted = hits(sp_v[p, 0:1], sp_v[p, 1:2], counts_v[p], 0)
    counted = counted + is_edit * hits(mp_v[0:1], mp_v[1:2], counts_v[2], NZ)
    allowed = (counted > 0.5).astype(F32)
    spread = lax.broadcasted_iota(I32, (NX * SLOTS, QUERIES), 1) // TILE
    spread = (spread == lax.broadcasted_iota(I32, (NX * SLOTS, QUERIES), 0)).astype(F32)
    live = jnp.dot(allowed, spread, preferred_element_type=F32)
    bias[...] = jnp.where(live > 0.5, 0.0, NOTHING)
    tops[...] = jnp.full(tops.shape, NOTHING, F32)
    totals[...] = jnp.zeros(totals.shape, F32)
    acc[...] = jnp.zeros(acc.shape, F32)

    def chip_copy(r):
        return remote(kv.at[r], kv.at[NZ + r], c_send.at[r], c_recv.at[r], dev(core=1 - p))

    pl.when(p == 0)(chip_copy(z).start)

    def pass_on(i):
        r = row_order(i, z)
        place = kv.at[r]
        arriving = two_copies(r, place, z_send, 0, dev())
        up, down = up_copy(r, place, zf_send, r), down_copy(r, place, zf_send, r)
        for k in range(2):
            arriving.copies[k].wait_recv()
            pl.when((r < z) & (z < b))(up.copies[k].start)
            pl.when((r > z) & (z > a))(down.copies[k].start)
        pl.when(p == 0)(chip_copy(r).start)

    def qx_copy(j, d):
        place = qs.at[j * NX + x]
        return remote(place, place, qx_send.at[3 * j + d - 1], qx_recv.at[3 * j + d - 1], along_x(d))

    def qx_arrival(j, d):
        place = qs.at[j * NX + (x + NX - d) % NX]
        return remote(place, place, qx_send.at[3 * j + d - 1], qx_recv.at[3 * j + d - 1], along_x(d))

    def live_slot(j):
        row = slot_row(z, g, j)
        return row, (row >= 0) & (row < NZ)

    for n in range(3):
        row, away, here = query_copies(n)
        pl.when(row == z)(here.wait)

    for j in range(SLOTS):
        row, live = live_slot(j)
        place = qs.at[j * NX + x]

        @pl.when(live)
        def _():
            pl.when(row != z)(remote(place, place, q_send.at[0], q_recv.at[j], dev()).wait_recv)
            for d in (2, 1, 3):
                qx_copy(j, d).start()

    pass_on(1)

    pass_on(2)

    @pl.when(p == 0)
    def _():
        for n in range(2):
            pl.when((g == 1) == (n == 0))(entry_copy(n)[1].wait_send)
        pl.semaphore_signal(turn, inc=1, device_id=dev(core=1), device_id_type=MESH)

        def passing(i, carry):
            pass_on(i)
            return carry

        lax.fori_loop(3, NZ, passing, 0)

    @pl.when(p == 1)
    def _():
        pl.semaphore_wait(turn, 1)
        for n in range(3):
            e, copy = entry_copy(n)
            pl.when(later(e))(copy.start)

    for j in range(SLOTS):
        row, live = live_slot(j)

        @pl.when(live)
        def _():
            for d in range(1, NX):
                qx_arrival(j, d).wait_recv()
            for xx in range(NX):
                at = j * NX + xx
                qt[:, at * TILE:(at + 1) * TILE] = qs[at].T

    live_slots = jnp.where(g == 1, 4, jnp.where((z == 2) | (z == 5), 2, 3))

    def attend(r, u, base):
        for width in range(2, SLOTS + 1):
            pl.when(live_slots == width)(functools.partial(attend_slots, r, u, base, width * NX * TILE))

    def attend_slots(r, u, base, width):
        cols = slice(0, width)
        keys = jnp.concatenate([kv[base + r, :TILE, :], kv[base + u, :TILE, :]], axis=0)
        values = jnp.concatenate([kv[base + r, TILE:, :], kv[base + u, TILE:, :]], axis=1)
        scores = jnp.dot(keys, qt[:, cols], preferred_element_type=F32)
        first, second = scores[:TILE], scores[TILE:]
        first_bias = bias[pl.ds(base + r, 1), cols]
        second_bias = bias[pl.ds(base + u, 1), cols]
        top = tops[:, cols]
        new_top = jnp.maximum(top, jnp.maximum(
            jnp.max(first, axis=0, keepdims=True) * EXP2_SCALE + first_bias,
            jnp.max(second, axis=0, keepdims=True) * EXP2_SCALE + second_bias,
        ))
        level = jnp.maximum(new_top, NOTHING / 10)
        faded = jnp.exp2(top - new_top)
        first = jnp.exp2(first * EXP2_SCALE - (level - first_bias))
        second = jnp.exp2(second * EXP2_SCALE - (level - second_bias))
        tops[:, cols] = new_top
        totals[:, cols] = totals[:, cols] * faded + jnp.sum((first + second).reshape(16, 8, width), axis=0)
        weights = jnp.concatenate([first.astype(BF16), second.astype(BF16)], axis=0)
        acc[:, cols] = acc[:, cols] * faded + jnp.dot(values, weights, preferred_element_type=F32)

    def step(i, carry):
        cross = (i != 1) & (i < 5)
        at = jnp.where(i < 2, 0, jnp.where(i < 5, i - 1, i - 4))
        r, u = row_order(2 * at, z), row_order(2 * at + 1, z)

        @pl.when(cross & (p == 1))
        def _():
            chip_copy(r).wait_recv()
            chip_copy(u).wait_recv()
            attend(r, u, NZ)

        @pl.when(jnp.logical_not(cross))
        def _():
            @pl.when((at > 0) & (p == 1))
            def _():
                pl.when(at > 1)(lambda: pass_on(2 * at))
                pass_on(2 * at + 1)

            attend(r, u, 0)

        return carry

    lax.fori_loop(0, NZ, step, 0)

    whole = jnp.sum(totals[...], axis=0, keepdims=True)
    some = whole > 0.0
    inverse = 1.0 / jnp.where(some, whole, 1.0)
    level = jnp.where(some, tops[...] + jnp.log2(jnp.where(some, whole, 1.0)), NOTHING)
    for j in range(SLOTS):
        for xx in range(NX):
            at = j * NX + xx
            cols = slice(at * TILE, (at + 1) * TILE)
            stat_v[xx, j:j + 1, :] = level[:, cols]

    def stat_copy(d):
        return remote(
            stat_v.at[(x + d) % NX], part_stats.at[d - 1], s_send.at[d - 1], s_recv.at[d - 1], along_x(d)
        )

    def part_copy(j, d):
        at = 3 * j + d - 1
        return remote(
            o_v.at[j * NX + (x + d) % NX], parts.at[at], x_send.at[at], x_recv.at[at], along_x(d)
        )

    for d in range(1, NX):
        stat_copy(d).start()
    for j in range(SLOTS):
        row, live = live_slot(j)

        @pl.when(live)
        def _():
            for xx in range(NX):
                at = j * NX + xx
                cols = slice(at * TILE, (at + 1) * TILE)
                o_v[at] = (acc[:, cols] * inverse[:, cols]).astype(BF16)
            for d in (2, 1, 3):
                part_copy(j, d).start()

    for d in range(1, NY):
        for part in range(2):
            w_arrival(d, part).wait_recv()
        w_swap(d, rows_mine).start()

    def back(j):
        row, live = live_slot(j)
        dst = full.at[3 * y + g]
        away = remote(merged.at[j], dst, o_send.at[j], o_recv.at[g], dev(seq=x * NZ + row))
        here = pltpu.make_async_copy(merged.at[j], dst, o_send.at[j])
        return row, live, away, here

    for d in range(1, NX):
        stat_copy(d).wait_recv()
    for j in range(SLOTS):
        row, live, away, here = back(j)

        @pl.when(live)
        def _():
            stats = [stat_v[x, j:j + 1, :]] + [part_stats[d, j:j + 1, :] for d in range(3)]
            top = functools.reduce(jnp.maximum, stats)
            shares = [jnp.exp2(stat - top) for stat in stats]
            share_sum = sum(shares)
            for d in range(1, NX):
                part_copy(j, d).wait_recv()
            blocks = [o_v[j * NX + x]] + [parts[3 * j + d] for d in range(3)]
            mixed = sum(block.astype(F32) * (share / share_sum) for block, share in zip(blocks, shares))
            merged[j] = mixed.T.astype(BF16)
            pl.when(row != z)(away.start)
            pl.when(row == z)(here.start)

    def y_copy(n, d):
        block = full.at[3 * y + n]
        return remote(block, block, y_send.at[3 * n + d - 1], y_recv.at[3 * n + d - 1], along_y(d))

    def y_arrival(n, d):
        block = full.at[3 * ((y + NY - d) % NY) + n]
        return remote(block, block, y_send.at[3 * n + d - 1], y_recv.at[3 * n + d - 1], along_y(d))

    for j in range(SLOTS):
        row, live, away, here = back(j)
        pl.when(live & (row == z))(here.wait)

    for n in range(3):
        row, _slot = query_place(z, n)
        block = full.at[3 * y + n]
        pl.when(row != z)(remote(block, block, o_send.at[0], o_recv.at[n], dev()).wait_recv)
        for d in (2, 1, 3):
            y_copy(n, d).start()

    for load in loads[6:]:
        load.wait()
    for d in range(1, NY):
        w_swap(d, rows_other).wait_recv()
    def projected(n, d, part):
        at = (y + NY - d) % NY
        return jnp.dot(
            full[3 * at + n], w_v[at, n * HD:(n + 1) * HD, part_cols(part)], preferred_element_type=F32
        )

    theirs = sum(projected(n, 0, 1) for n in range(3))
    for n in range(3):
        for d in range(1, NY):
            y_arrival(n, d).wait_recv()
            theirs = theirs + projected(n, d, 1)
    give[...] = theirs.astype(BF16)
    swap = remote(give, got, h_send, h_recv, partner)
    swap.start()
    own = sum(projected(n, d, 0) for n in range(3) for d in range(NY))
    swap.wait_recv()
    out_ref[...] = (own + got[...].astype(F32)).astype(BF16)

    def drain(r, carry):
        place = kv.at[r]
        pl.when((r < z) & (z < b))(up_copy(r, place, zf_send, r).wait_send)
        pl.when((r > z) & (z > a))(down_copy(r, place, zf_send, r).wait_send)
        pl.when(p == 0)(chip_copy(r).wait_send)
        return carry

    lax.fori_loop(0, NZ, drain, 0)
    pl.when(z < b)(up_copy(z, mine.at[g], z_send, 3).wait_send)
    pl.when(z > a)(down_copy(z, mine.at[g], z_send, 4).wait_send)
    for n in range(3):
        e, copy = entry_copy(n)
        waited = (p == 0) & ((g == 1) if n == 0 else (g != 1) & (n == 1))
        pl.when((e != z) & jnp.logical_not(waited))(copy.wait_send)
        row, away, here = query_copies(n)
        pl.when(row != z)(away.wait_send)

    for j in range(SLOTS):
        row, live, away, here = back(j)

        @pl.when(live)
        def _():
            for d in range(1, NX):
                qx_copy(j, d).wait_send()
                part_copy(j, d).wait_send()
            pl.when(row != z)(away.wait_send)

    for d in range(1, NX):
        stat_copy(d).wait_send()
    for d in range(1, NY):
        for part in range(2):
            w_copy(d, part).wait_send()
        w_swap(d, rows_mine).wait_send()
        for n in range(3):
            y_copy(n, d).wait_send()
    swap.wait_send()


def on_device(queries, keys, values, self_pairs, mask_pairs, counts, out_weight):
    hbm = pl.BlockSpec(memory_space=pltpu.HBM)
    vmem = pltpu.VMEM
    dma = pltpu.SemaphoreType.DMA
    rows = (TILE, 3 * HD)
    projected = pl.pallas_call(
        layer_kernel,
        out_shape=jax.ShapeDtypeStruct(rows, BF16),
        in_specs=[hbm] * 7,
        out_specs=pl.BlockSpec(memory_space=vmem),
        scratch_shapes=[
            vmem(rows, BF16), vmem(rows, BF16), vmem(rows, BF16),
            vmem((2, 2, self_pairs.shape[1]), I32), vmem((2, mask_pairs.shape[0]), I32), pltpu.SMEM((3,), I32),
            vmem((3, 2 * TILE, HD), BF16),
            vmem((ENTRIES, 2 * TILE, HD), BF16),
            vmem((NX * SLOTS, TILE, HD), BF16),
            vmem((HD, QUERIES), BF16),
            vmem((ENTRIES, QUERIES), F32),
            vmem((1, QUERIES), F32),
            vmem((8, QUERIES), F32),
            vmem((HD, QUERIES), F32),
            vmem((NY, 3 * HD, 6 * HD), BF16),
            vmem((NX * SLOTS, HD, TILE), BF16),
            vmem((NX, 8, TILE), F32),
            vmem((3 * SLOTS, HD, TILE), BF16),
            vmem((3, 8, TILE), F32),
            vmem((SLOTS, TILE, HD), BF16),
            vmem((3 * NY, TILE, HD), BF16),
            vmem(rows, BF16), vmem(rows, BF16),
            dma((10,)), dma((2 * NZ,)), dma((2 * NZ,)), dma((NZ,)), dma((NZ,)),
            dma((3,)), dma((SLOTS,)), dma((3 * SLOTS,)), dma((3 * SLOTS,)),
            dma((2 * NY,)), dma((2 * NY,)), dma((NY,)), dma((NY,)),
            dma((3 * SLOTS,)), dma((3 * SLOTS,)), dma((3,)), dma((3,)),
            dma((SLOTS,)), dma((3,)), dma((9,)), dma((9,)), dma, dma, pltpu.SemaphoreType.REGULAR, dma((8,)),
        ],
        compiler_params=pltpu.CompilerParams(
            collective_id=0, has_side_effects=True, vmem_limit_bytes=32 * 1024 * 1024
        ),
        name="layer",
    )(*[
        pltpu.with_memory_space_constraint(each, pltpu.HBM)
        for each in (
            counts, queries[0], keys[0], values[0],
            jnp.swapaxes(self_pairs, 1, 2), jnp.swapaxes(mask_pairs, 0, 1), out_weight,
        )
    ])
    return projected[None]


def solution(mesh):
    in_specs = (
        P("pass", "seq", "head"),
        P("pass", "seq", "head"),
        P("pass", "seq", "head"),
        P(),
        P(),
        P(),
        P("head", None),
    )
    out_specs = P("pass", "seq", "head")
    return jax.shard_map(
        on_device, mesh=mesh, in_specs=in_specs, out_specs=out_specs, check_vma=False
    )
```

```python
import functools
import math

import jax
import jax.numpy as jnp
from jax import lax
from jax.experimental import pallas as pl
from jax.experimental.pallas import tpu as pltpu
from jax.sharding import PartitionSpec as P

HD = 128
TILE = 128
NX = 4
NZ = 8
NY = 4
SLOTS = 4
ENTRIES = 2 * NZ
BF16 = jnp.bfloat16
F32 = jnp.float32
I32 = jnp.int32
EXP2_SCALE = HD ** -0.5 * math.log2(math.e)
NOTHING = -1e30
QUERIES = NX * SLOTS * TILE
MESH = pl.DeviceIdType.MESH


def head_of_row(z):
    return (3 * z + 1) // 8


def first_row(g):
    return (8 * g + 1) // 3


def last_row(g):
    return (8 * g + 9) // 3 - 1


def query_place(zq, g):
    if g == 0:
        return zq // 3, zq % 3
    if g == 1:
        return 3 + zq // 4, zq % 4
    return 7 - (7 - zq) // 3, (7 - zq) % 3


def slot_row(z, g, j):
    low = 3 * z + j
    mid = 4 * (z - 3) + j
    high = 7 - (3 * (7 - z) + j)
    row = jnp.where(g == 0, low, jnp.where(g == 1, mid, high))
    return jnp.where((j == 3) & (g != 1), -1, row)


def row_order(i, z):
    near = jnp.minimum(z, 7 - z)
    d = (i + 1) // 2
    both = z + d * (1 - 2 * (i % 2))
    return jnp.where(i <= 2 * near, both, jnp.where(z <= 3, i, 7 - i))


def remote(src, dst, send, recv, target):
    return pltpu.make_async_remote_copy(
        src_ref=src, dst_ref=dst, send_sem=send, recv_sem=recv, device_id=target, device_id_type=MESH
    )


class Copies:
    def __init__(self, copies):
        self.copies = copies

    def start(self):
        for copy in self.copies:
            copy.start()

    def wait_send(self):
        for copy in self.copies:
            copy.wait_send()


def layer_kernel(
    counts_ref, q_ref, k_ref, v_ref, sp_ref, mp_ref, w_ref, out_ref,
    q_v, k_v, v_v, sp_v, mp_v, counts_v,
    mine, kv, qs, qt, bias, tops, totals, acc, w_v,
    o_v, stat_v, parts, part_stats, merged, full, give, got,
    z_send, z_recv, zf_send, c_send, c_recv,
    q_send, q_recv, qx_send, qx_recv, w_send, w_recv, wc_send, wc_recv,
    x_send, x_recv, s_send, s_recv, o_send, o_recv, y_send, y_recv, h_send, h_recv, turn, local_sem,
):
    s = lax.axis_index("seq")
    p = lax.axis_index("pass")
    h = lax.axis_index("head")
    x, z = s // NZ, s % NZ
    zh, y = h // NY, h % NY
    g = head_of_row(z)
    a, b = first_row(g), last_row(g)

    def dev(seq=s, core=p, head=h):
        return {"seq": seq, "pass": core, "head": head}

    def along_x(d):
        return dev(seq=((x + d) % NX) * NZ + z)

    def along_y(d):
        return dev(head=zh * NY + (y + d) % NY)

    partner = dev(head=(1 - zh) * NY + y)
    met = (
        [dev(seq=x * NZ + (z + d) % NZ) for d in range(1, NZ)]
        + [along_x(d) for d in range(1, NX)]
        + [along_y(d) for d in range(1, NY)]
        + [dev(core=1 - p), partner]
    )
    barrier = pltpu.get_barrier_semaphore()
    for device in met:
        pl.semaphore_signal(barrier, inc=1, device_id=device, device_id_type=MESH)

    def w_cols(yy, part):
        zz = zh if part == 0 else 1 - zh
        return pl.ds(pl.multiple_of((zz * NY + yy) * (3 * HD), 3 * HD), 3 * HD)

    def part_cols(part):
        return slice(part * 3 * HD, (part + 1) * 3 * HD)

    loads = [
        pltpu.make_async_copy(src, dst, local_sem.at[i])
        for i, (src, dst) in enumerate(
            [(k_ref, k_v), (v_ref, v_v), (q_ref, q_v), (counts_ref, counts_v), (sp_ref, sp_v), (mp_ref, mp_v)]
            + [(w_ref.at[:, w_cols(y, part)], w_v.at[y, :, part_cols(part)]) for part in range(2)]
        )
    ]
    for load in loads:
        load.start()

    loads[0].wait()
    loads[1].wait()
    for n in range(3):
        cols = slice(n * HD, (n + 1) * HD)
        mine[n, :TILE, :] = k_v[:, cols]
        mine[n, TILE:, :] = v_v[:, cols].T
    kv[z] = mine[g]
    loads[2].wait()

    pl.semaphore_wait(barrier, len(met))

    def query_copies(n):
        row, slot = query_place(z, n)
        src, dst = q_v.at[:, n * HD:(n + 1) * HD], qs.at[slot * NX + x]
        away = remote(src, dst, q_send.at[n], q_recv.at[slot], dev(seq=x * NZ + row))
        here = pltpu.make_async_copy(src, dst, q_send.at[n])
        return row, away, here

    for n in range(3):
        row, away, here = query_copies(n)
        pl.when(row != z)(away.start)
        pl.when(row == z)(here.start)

    def two_copies(r, src, sems, at, target):
        return Copies([
            remote(src.at[part], kv.at[r].at[part], sems.at[2 * at + k], z_recv.at[2 * r + k], target)
            for k, part in enumerate((slice(0, TILE), slice(TILE, 2 * TILE)))
        ])

    def up_copy(r, src, sems, at):
        return two_copies(r, src, sems, at, dev(seq=s + 1))

    def down_copy(r, src, sems, at):
        return two_copies(r, src, sems, at, dev(seq=s - 1))

    def entry_copy(n):
        e = jnp.maximum(first_row(n), jnp.minimum(z, last_row(n)))
        return e, two_copies(z, mine.at[n], z_send, n, dev(seq=x * NZ + e))

    pl.when(z < b)(up_copy(z, mine.at[g], z_send, 3).start)
    pl.when(z > a)(down_copy(z, mine.at[g], z_send, 4).start)
    def later(e):
        return (p == 1) & ((e - z) * (e - z) > 1)

    for n in range(3):
        e, copy = entry_copy(n)
        pl.when((e != z) & jnp.logical_not(later(e)))(copy.start)

    half_rows = 3 * HD // 2
    rows_mine = pl.ds(pl.multiple_of(p * half_rows, half_rows), half_rows)
    rows_other = pl.ds(pl.multiple_of((1 - p) * half_rows, half_rows), half_rows)

    def w_copy(d, part):
        return remote(
            w_ref.at[rows_mine, w_cols((y + d) % NY, part)], w_v.at[y, rows_mine, part_cols(part)],
            w_send.at[2 * d + part], w_recv.at[2 * d + part], along_y(d),
        )

    def w_arrival(d, part):
        place = w_v.at[(y + NY - d) % NY, rows_mine, part_cols(part)]
        return remote(place, place, w_send.at[2 * d + part], w_recv.at[2 * d + part], along_y(d))

    def w_swap(d, rows):
        place = w_v.at[(y + NY - d) % NY, rows]
        return remote(place, place, wc_send.at[d], wc_recv.at[d], dev(core=1 - p))

    for part in range(2):
        for d in range(1, NY):
            w_copy(d, part).start()

    for load in loads[3:6]:
        load.wait()
    slots = lax.broadcasted_iota(I32, (NX * SLOTS, 1), 0)
    tiles = jnp.full((NX * SLOTS, 1), -1, I32)
    for j in range(SLOTS):
        row = slot_row(z, g, j)
        live = (row >= 0) & (row < NZ)
        tiles = jnp.where(((slots >> 2) == j) & live, (slots & 3) * NZ + row, tiles)

    def hits(queries, keys, live_count, shift):
        live = lax.broadcasted_iota(I32, queries.shape, 1) < live_count
        row_hits = ((queries == tiles) & live).astype(F32)
        row = keys - x * NZ
        row = jnp.where((row >= 0) & (row < NZ), row + shift, -1)
        col_hits = (lax.broadcasted_iota(I32, (ENTRIES, 1), 0) == row).astype(F32)
        return lax.dot_general(col_hits, row_hits, (((1,), (1,)), ((), ())), preferred_element_type=F32)

    is_edit = (p == 1).astype(F32)
    counted = hits(sp_v[p, 0:1], sp_v[p, 1:2], counts_v[p], 0)
    counted = counted + is_edit * hits(mp_v[0:1], mp_v[1:2], counts_v[2], NZ)
    allowed = (counted > 0.5).astype(F32)
    spread = lax.broadcasted_iota(I32, (NX * SLOTS, QUERIES), 1) // TILE
    spread = (spread == lax.broadcasted_iota(I32, (NX * SLOTS, QUERIES), 0)).astype(F32)
    live = jnp.dot(allowed, spread, preferred_element_type=F32)
    bias[...] = jnp.where(live > 0.5, 0.0, NOTHING)
    tops[...] = jnp.full(tops.shape, NOTHING, F32)
    totals[...] = jnp.zeros(totals.shape, F32)
    acc[...] = jnp.zeros(acc.shape, F32)

    def chip_copy(r):
        return remote(kv.at[r], kv.at[NZ + r], c_send.at[r], c_recv.at[r], dev(core=1 - p))

    pl.when(p == 0)(chip_copy(z).start)

    def pass_on(i):
        r = row_order(i, z)
        place = kv.at[r]
        arriving = two_copies(r, place, z_send, 0, dev())
        up, down = up_copy(r, place, zf_send, r), down_copy(r, place, zf_send, r)
        for k in range(2):
            arriving.copies[k].wait_recv()
            pl.when((r < z) & (z < b))(up.copies[k].start)
            pl.when((r > z) & (z > a))(down.copies[k].start)
        pl.when(p == 0)(chip_copy(r).start)

    def qx_copy(j, d):
        place = qs.at[j * NX + x]
        return remote(place, place, qx_send.at[3 * j + d - 1], qx_recv.at[3 * j + d - 1], along_x(d))

    def qx_arrival(j, d):
        place = qs.at[j * NX + (x + NX - d) % NX]
        return remote(place, place, qx_send.at[3 * j + d - 1], qx_recv.at[3 * j + d - 1], along_x(d))

    def live_slot(j):
        row = slot_row(z, g, j)
        return row, (row >= 0) & (row < NZ)

    for n in range(3):
        row, away, here = query_copies(n)
        pl.when(row == z)(here.wait)

    for j in range(SLOTS):
        row, live = live_slot(j)
        place = qs.at[j * NX + x]

        @pl.when(live)
        def _():
            pl.when(row != z)(remote(place, place, q_send.at[0], q_recv.at[j], dev()).wait_recv)
            for d in (2, 1, 3):
                qx_copy(j, d).start()

    pass_on(1)

    pass_on(2)

    @pl.when(p == 0)
    def _():
        for n in range(2):
            pl.when((g == 1) == (n == 0))(entry_copy(n)[1].wait_send)
        pl.semaphore_signal(turn, inc=1, device_id=dev(core=1), device_id_type=MESH)

        def passing(i, carry):
            pass_on(i)
            return carry

        lax.fori_loop(3, NZ, passing, 0)

    @pl.when(p == 1)
    def _():
        pl.semaphore_wait(turn, 1)
        for n in range(3):
            e, copy = entry_copy(n)
            pl.when(later(e))(copy.start)

    for j in range(SLOTS):
        row, live = live_slot(j)

        @pl.when(live)
        def _():
            for d in range(1, NX):
                qx_arrival(j, d).wait_recv()
            for xx in range(NX):
                at = j * NX + xx
                qt[:, at * TILE:(at + 1) * TILE] = qs[at].T

    live_slots = jnp.where(g == 1, 4, jnp.where((z == 2) | (z == 5), 2, 3))

    def attend(r, u, base):
        for width in range(2, SLOTS + 1):
            pl.when(live_slots == width)(functools.partial(attend_slots, r, u, base, width * NX * TILE))

    def attend_slots(r, u, base, width):
        cols = slice(0, width)
        keys = jnp.concatenate([kv[base + r, :TILE, :], kv[base + u, :TILE, :]], axis=0)
        values = jnp.concatenate([kv[base + r, TILE:, :], kv[base + u, TILE:, :]], axis=1)
        scores = jnp.dot(keys, qt[:, cols], preferred_element_type=F32)
        first, second = scores[:TILE], scores[TILE:]
        first_bias = bias[pl.ds(base + r, 1), cols]
        second_bias = bias[pl.ds(base + u, 1), cols]
        top = tops[:, cols]
        new_top = jnp.maximum(top, jnp.maximum(
            jnp.max(first, axis=0, keepdims=True) * EXP2_SCALE + first_bias,
            jnp.max(second, axis=0, keepdims=True) * EXP2_SCALE + second_bias,
        ))
        level = jnp.maximum(new_top, NOTHING / 10)
        faded = jnp.exp2(top - new_top)
        first = jnp.exp2(first * EXP2_SCALE - (level - first_bias))
        second = jnp.exp2(second * EXP2_SCALE - (level - second_bias))
        tops[:, cols] = new_top
        totals[:, cols] = totals[:, cols] * faded + jnp.sum((first + second).reshape(16, 8, width), axis=0)
        weights = jnp.concatenate([first.astype(BF16), second.astype(BF16)], axis=0)
        acc[:, cols] = acc[:, cols] * faded + jnp.dot(values, weights, preferred_element_type=F32)

    def step(i, carry):
        cross = (i != 1) & (i < 5)
        at = jnp.where(i < 2, 0, jnp.where(i < 5, i - 1, i - 4))
        r, u = row_order(2 * at, z), row_order(2 * at + 1, z)

        @pl.when(cross & (p == 1))
        def _():
            chip_copy(r).wait_recv()
            chip_copy(u).wait_recv()

        @pl.when(jnp.logical_not(cross) & (at > 0) & (p == 1))
        def _():
            pl.when(at > 1)(lambda: pass_on(2 * at))
            pass_on(2 * at + 1)

        pl.when(jnp.logical_not(cross) | (p == 1))(lambda: attend(r, u, jnp.where(cross, NZ, 0)))
        return carry

    lax.fori_loop(0, NZ, step, 0)

    whole = jnp.sum(totals[...], axis=0, keepdims=True)
    some = whole > 0.0
    inverse = 1.0 / jnp.where(some, whole, 1.0)
    level = jnp.where(some, tops[...] + jnp.log2(jnp.where(some, whole, 1.0)), NOTHING)
    for j in range(SLOTS):
        for xx in range(NX):
            at = j * NX + xx
            cols = slice(at * TILE, (at + 1) * TILE)
            stat_v[xx, j:j + 1, :] = level[:, cols]

    def stat_copy(d):
        return remote(
            stat_v.at[(x + d) % NX], part_stats.at[d - 1], s_send.at[d - 1], s_recv.at[d - 1], along_x(d)
        )

    def part_copy(j, d):
        at = 3 * j + d - 1
        return remote(
            o_v.at[j * NX + (x + d) % NX], parts.at[at], x_send.at[at], x_recv.at[at], along_x(d)
        )

    for d in range(1, NX):
        stat_copy(d).start()
    for j in range(SLOTS):
        row, live = live_slot(j)

        @pl.when(live)
        def _():
            for xx in range(NX):
                at = j * NX + xx
                cols = slice(at * TILE, (at + 1) * TILE)
                o_v[at] = (acc[:, cols] * inverse[:, cols]).astype(BF16)
            for d in (2, 1, 3):
                part_copy(j, d).start()

    for d in range(1, NY):
        for part in range(2):
            w_arrival(d, part).wait_recv()
        w_swap(d, rows_mine).start()

    def back(j):
        row, live = live_slot(j)
        dst = full.at[3 * y + g]
        away = remote(merged.at[j], dst, o_send.at[j], o_recv.at[g], dev(seq=x * NZ + row))
        return row, live, away

    for d in range(1, NX):
        stat_copy(d).wait_recv()
    for j in range(SLOTS):
        row, live, away = back(j)

        @pl.when(live)
        def _():
            stats = [stat_v[x, j:j + 1, :]] + [part_stats[d, j:j + 1, :] for d in range(3)]
            top = functools.reduce(jnp.maximum, stats)
            shares = [jnp.exp2(stat - top) for stat in stats]
            share_sum = sum(shares)
            for d in range(1, NX):
                part_copy(j, d).wait_recv()
            blocks = [o_v[j * NX + x]] + [parts[3 * j + d] for d in range(3)]
            mixed = sum(block.astype(F32) * (share / share_sum) for block, share in zip(blocks, shares))
            tile = mixed.T.astype(BF16)

            @pl.when(row == z)
            def _():
                full[3 * y + g] = tile

            @pl.when(row != z)
            def _():
                merged[j] = tile
                away.start()

    def y_copy(n, d):
        block = full.at[3 * y + n]
        return remote(block, block, y_send.at[3 * n + d - 1], y_recv.at[3 * n + d - 1], along_y(d))

    def y_arrival(n, d):
        block = full.at[3 * ((y + NY - d) % NY) + n]
        return remote(block, block, y_send.at[3 * n + d - 1], y_recv.at[3 * n + d - 1], along_y(d))

    for n in range(3):
        row, _slot = query_place(z, n)
        block = full.at[3 * y + n]
        pl.when(row != z)(remote(block, block, o_send.at[0], o_recv.at[n], dev()).wait_recv)
        for d in (2, 1, 3):
            y_copy(n, d).start()

    for load in loads[6:]:
        load.wait()
    for d in range(1, NY):
        w_swap(d, rows_other).wait_recv()
    def projected(n, d, part):
        at = (y + NY - d) % NY
        return jnp.dot(
            full[3 * at + n], w_v[at, n * HD:(n + 1) * HD, part_cols(part)], preferred_element_type=F32
        )

    theirs = sum(projected(n, 0, 1) for n in range(3))
    for n in range(3):
        for d in range(1, NY):
            y_arrival(n, d).wait_recv()
            theirs = theirs + projected(n, d, 1)
    give[...] = theirs.astype(BF16)
    swap = remote(give, got, h_send, h_recv, partner)
    swap.start()
    own = sum(projected(n, d, 0) for n in range(3) for d in range(NY))
    swap.wait_recv()
    out_ref[...] = (own + got[...].astype(F32)).astype(BF16)

    def drain(r, carry):
        place = kv.at[r]
        pl.when((r < z) & (z < b))(up_copy(r, place, zf_send, r).wait_send)
        pl.when((r > z) & (z > a))(down_copy(r, place, zf_send, r).wait_send)
        pl.when(p == 0)(chip_copy(r).wait_send)
        return carry

    lax.fori_loop(0, NZ, drain, 0)
    pl.when(z < b)(up_copy(z, mine.at[g], z_send, 3).wait_send)
    pl.when(z > a)(down_copy(z, mine.at[g], z_send, 4).wait_send)
    for n in range(3):
        e, copy = entry_copy(n)
        waited = (p == 0) & ((g == 1) if n == 0 else (g != 1) & (n == 1))
        pl.when((e != z) & jnp.logical_not(waited))(copy.wait_send)
        row, away, here = query_copies(n)
        pl.when(row != z)(away.wait_send)

    for j in range(SLOTS):
        row, live, away = back(j)

        @pl.when(live)
        def _():
            for d in range(1, NX):
                qx_copy(j, d).wait_send()
                part_copy(j, d).wait_send()
            pl.when(row != z)(away.wait_send)

    for d in range(1, NX):
        stat_copy(d).wait_send()
    for d in range(1, NY):
        for part in range(2):
            w_copy(d, part).wait_send()
        w_swap(d, rows_mine).wait_send()
        for n in range(3):
            y_copy(n, d).wait_send()
    swap.wait_send()


def on_device(queries, keys, values, self_pairs, mask_pairs, counts, out_weight):
    hbm = pl.BlockSpec(memory_space=pltpu.HBM)
    vmem = pltpu.VMEM
    dma = pltpu.SemaphoreType.DMA
    rows = (TILE, 3 * HD)
    projected = pl.pallas_call(
        layer_kernel,
        out_shape=jax.ShapeDtypeStruct(rows, BF16),
        in_specs=[hbm] * 7,
        out_specs=pl.BlockSpec(memory_space=vmem),
        scratch_shapes=[
            vmem(rows, BF16), vmem(rows, BF16), vmem(rows, BF16),
            vmem((2, 2, self_pairs.shape[1]), I32), vmem((2, mask_pairs.shape[0]), I32), pltpu.SMEM((3,), I32),
            vmem((3, 2 * TILE, HD), BF16),
            vmem((ENTRIES, 2 * TILE, HD), BF16),
            vmem((NX * SLOTS, TILE, HD), BF16),
            vmem((HD, QUERIES), BF16),
            vmem((ENTRIES, QUERIES), F32),
            vmem((1, QUERIES), F32),
            vmem((8, QUERIES), F32),
            vmem((HD, QUERIES), F32),
            vmem((NY, 3 * HD, 6 * HD), BF16),
            vmem((NX * SLOTS, HD, TILE), BF16),
            vmem((NX, 8, TILE), F32),
            vmem((3 * SLOTS, HD, TILE), BF16),
            vmem((3, 8, TILE), F32),
            vmem((SLOTS, TILE, HD), BF16),
            vmem((3 * NY, TILE, HD), BF16),
            vmem(rows, BF16), vmem(rows, BF16),
            dma((10,)), dma((2 * NZ,)), dma((2 * NZ,)), dma((NZ,)), dma((NZ,)),
            dma((3,)), dma((SLOTS,)), dma((3 * SLOTS,)), dma((3 * SLOTS,)),
            dma((2 * NY,)), dma((2 * NY,)), dma((NY,)), dma((NY,)),
            dma((3 * SLOTS,)), dma((3 * SLOTS,)), dma((3,)), dma((3,)),
            dma((SLOTS,)), dma((3,)), dma((9,)), dma((9,)), dma, dma, pltpu.SemaphoreType.REGULAR, dma((8,)),
        ],
        compiler_params=pltpu.CompilerParams(
            collective_id=0, has_side_effects=True, vmem_limit_bytes=32 * 1024 * 1024
        ),
        name="layer",
    )(*[
        pltpu.with_memory_space_constraint(each, pltpu.HBM)
        for each in (
            counts, queries[0], keys[0], values[0],
            jnp.swapaxes(self_pairs, 1, 2), jnp.swapaxes(mask_pairs, 0, 1), out_weight,
        )
    ])
    return projected[None]


def solution(mesh):
    in_specs = (
        P("pass", "seq", "head"),
        P("pass", "seq", "head"),
        P("pass", "seq", "head"),
        P(),
        P(),
        P(),
        P("head", None),
    )
    out_specs = P("pass", "seq", "head")
    return jax.shard_map(
        on_device, mesh=mesh, in_specs=in_specs, out_specs=out_specs, check_vma=False
    )
```
